1024 devices in a mesh: sx: 16 (over y, x_hi), sy: 64 (over z, x_lo, core).
Axes of the slice: x: 4 (x_hi: 2, x_lo: 2; x = x_hi * 2 + x_lo), y: 8, z: 16, core: 2. Of those that a mesh axis runs over, the one named last changes fastest.
Arguments:
- traces: bfloat16 [16, 64, 4, 6, 16, 768], P('sx', 'sy'), may hold values from -6 to 6
- viscosity: float32 [16, 64, 4], P('sx', 'sy'), may hold values from 0.1 to 10
- partner: int32 [16, 64, 4, 4], P('sx', 'sy'), may hold values from 0 to 3, as said below
- corner_owner: int32 [16, 64, 4, 8], P('sx', 'sy'), may hold values from 0 to 511
- self_block: bfloat16 [768, 768], replicated, may hold values from -0.21875 to 0.21875
- opposite_block: bfloat16 [768, 768], replicated, may hold values from -0.21875 to 0.21875
- cross_block: bfloat16 [768, 768], replicated, may hold values from -0.21875 to 0.21875
- corner_map: bfloat16 [24, 6, 768], replicated, may hold values from -0.09375 to 0.09375
Outputs:
- applied: float32 [16, 64, 4, 6, 16, 768], P('sx', 'sy')
- coarse: float32 [48, 8192], P(None, ('sx', 'sy'))
The draws below stay inside these ranges and needn't reach their ends.
Inputs may be any that keep to these rules, and one draw needn't show every extreme that they name: Face partners match: if the +x partner of (i, j, k) is slot p of (i+1, j), then the -x partner of (i+1, j, p) is slot k, likewise for y; each column of one device is a permutation of the 4 slots.
All inputs are finite; a program needn't handle non-finite values.
Results may differ from the reference program's by a relative error of at most 0.0042.
Values may be sent and summed in bfloat16 or wider, within the bound.
A program may use at most 32 MiB of HBM per device.

```python
import math
import jax
import jax.numpy as jnp
from jax import lax

FACE = 768
RHS = 16
SUB_DEV = 4
CORNERS = 8
COMPS = 3
SUB_X = 16
SUB_Y = 64
NC_ROW = 512


def draw_partner(key, part):
    key = jax.random.fold_in(key, 7)
    key_x, key_y = jax.random.split(key)
    slots = jnp.arange(SUB_DEV, dtype=jnp.int32)

    def one_perm(sub_key):
        scores = jax.random.randint(sub_key, (SUB_X, SUB_Y, SUB_DEV), 0, 1 << 20, dtype=jnp.int32)
        scores = scores * SUB_DEV + slots
        return jnp.argsort(scores, axis=-1).astype(jnp.int32)
    perm_x = one_perm(key_x)
    perm_y = one_perm(key_y)
    inverse_x = jnp.argsort(perm_x, axis=-1).astype(jnp.int32)
    inverse_y = jnp.argsort(perm_y, axis=-1).astype(jnp.int32)
    back_x = jnp.roll(inverse_x, 1, axis=0)
    back_y = jnp.roll(inverse_y, 1, axis=1)
    return jnp.stack([perm_x, back_x, perm_y, back_y], axis=-1).astype(jnp.int32)


def touch_ends(result, own_key, low, top_value):
    index_at = [jax.random.randint(jax.random.fold_in(own_key, axis), (), 0, length) for axis, length in enumerate(result.shape)]
    widest = result.shape.index(max(result.shape))
    beside = index_at[:widest] + [(index_at[widest] + 1) % result.shape[widest]] + index_at[widest + 1:]
    return result.at[tuple(index_at)].set(low).at[tuple(beside)].set(top_value)


def level_of(stream_key, extent, cuts, smallest, high):
    loudness, own = 1.0, jax.random.fold_in(stream_key, 6)
    for dim, shards_of in cuts:
        draws = jnp.exp(jax.random.uniform(jax.random.fold_in(own, dim), (shards_of,), jnp.float32, smallest / len(cuts), high / len(cuts)))
        loudness = loudness * jnp.repeat(draws, extent[dim] // shards_of).reshape([-1 if axis == dim else 1 for axis in range(len(extent))])
    return loudness


def bell_draw(key, dims, spread, reach, shards=(), kind=jnp.bfloat16):
    loudness = level_of(key, dims, shards, -0.22, 0.18) if shards else 1.0
    drawn = jax.random.normal(key, dims, jnp.float32) * spread * loudness
    return jnp.minimum(jnp.maximum(drawn, -reach), reach).astype(kind)


def setup_inputs(seed: int = 0) -> dict:
    seeds = jax.random.split(jax.random.key(seed), 9)
    return {
        "traces": bell_draw(seeds[0], (SUB_X, SUB_Y, SUB_DEV, 6, RHS, FACE), 1.0, 6.0, ((0, 16), (1, 64))),
        "viscosity": jnp.clip(jnp.exp(math.log(10.0) - 4.6051702 * jax.random.uniform(seeds[1], (SUB_X, SUB_Y, SUB_DEV), jnp.float32) ** level_of(seeds[1], (SUB_X, SUB_Y, SUB_DEV), ((0, 16), (1, 64)), -0.2, 0.2)), 0.1, 10.0),
        "partner": draw_partner(jax.random.fold_in(seeds[8], 71), 0),
        "corner_owner": touch_ends(jax.random.randint(seeds[3], (SUB_X, SUB_Y, SUB_DEV, CORNERS), 0, NC_ROW), jax.random.fold_in(seeds[3], 1), 0, NC_ROW - 1).astype(jnp.int32),
        "self_block": bell_draw(seeds[4], (FACE, FACE), FACE ** -0.5, 0.21875),
        "opposite_block": bell_draw(seeds[5], (FACE, FACE), FACE ** -0.5, 0.21875),
        "cross_block": bell_draw(seeds[6], (FACE, FACE), FACE ** -0.5, 0.21875),
        "corner_map": bell_draw(seeds[7], (CORNERS * COMPS, 6, FACE), (6 * FACE) ** -0.5, 0.09375),
    }


FLIP = (1, 0, 3, 2, 5, 4)


def facing(data, partner):
    zero_row = jnp.zeros_like(data[:1, :, :, 0])
    zero_col = jnp.zeros_like(data[:, :1, :, 0])
    zero_sub = jnp.zeros_like(data[:, :, :1, 0])
    up_x = jnp.concatenate([data[1:, :, :, 1], zero_row], 0)
    down_x = jnp.concatenate([zero_row, data[:-1, :, :, 0]], 0)
    up_y = jnp.concatenate([data[:, 1:, :, 3], zero_col], 1)
    down_y = jnp.concatenate([zero_col, data[:, :-1, :, 2]], 1)
    up_z = jnp.concatenate([data[:, :, 1:, 5], zero_sub], 2)
    down_z = jnp.concatenate([zero_sub, data[:, :, :-1, 4]], 2)

    def select(values, column):
        index = partner[:, :, :, column][:, :, :, None, None].astype(jnp.int32)
        return jnp.take_along_axis(values, index, axis=2)

    faces = [select(up_x, 0), select(down_x, 1), select(up_y, 2), select(down_y, 3), up_z, down_z]
    return jnp.stack(faces, axis=3)


def reference(traces, viscosity, partner, corner_owner, self_block, opposite_block, cross_block, corner_map):
    flip = jnp.array(FLIP, dtype=jnp.int32)
    jumps = (traces.astype(jnp.float32) - facing(traces, partner).astype(jnp.float32)).astype(jnp.bfloat16)
    width = self_block.shape[0]

    def row_work(inputs):
        jump_row, visc_row = inputs
        shape = jump_row.shape
        flat = jump_row.reshape(-1, width)
        with_self = jnp.dot(flat, self_block, preferred_element_type=jnp.float32).reshape(shape)
        with_opp = jnp.dot(flat, opposite_block, preferred_element_type=jnp.float32).reshape(shape)
        with_cross = jnp.dot(flat, cross_block, preferred_element_type=jnp.float32).reshape(shape)
        adjacent = jnp.sum(with_cross, axis=2, keepdims=True) - with_cross - jnp.take(with_cross, flip, axis=2)
        total = with_self + jnp.take(with_opp, flip, axis=2) + adjacent
        return (visc_row[:, :, None, None, None] * total).astype(jnp.bfloat16)

    local = lax.map(row_work, (jumps, viscosity))
    applied = local.astype(jnp.float32) - facing(local, partner).astype(jnp.float32)
    partials = jnp.einsum("xyzfqi,kfi->xyzqk", local.astype(jnp.float32), corner_map.astype(jnp.float32))
    rows = partials.shape[0]
    per_row = partials.reshape(rows, -1, RHS, CORNERS, COMPS)
    per_row = jnp.transpose(per_row, (0, 1, 3, 2, 4)).reshape(rows, -1, RHS * COMPS)
    owners = corner_owner.reshape(rows, -1).astype(jnp.int32)

    def assemble(inputs):
        values, ids = inputs
        return jnp.zeros((NC_ROW, RHS * COMPS), jnp.float32).at[ids].add(values)

    coarse = lax.map(assemble, (per_row, owners))
    coarse = jnp.transpose(coarse, (2, 0, 1)).reshape(RHS * COMPS, rows * NC_ROW)
    return applied, coarse
```

```python
import functools

import jax
import jax.numpy as jnp
from jax import lax
from jax.experimental import pallas as pl
from jax.experimental.pallas import tpu as pltpu
from jax.sharding import PartitionSpec as P

MESH = pl.DeviceIdType.MESH
F32, BF16 = jnp.float32, jnp.bfloat16
SUBS = 4
RHS = 16
HALF = 8
CORNERS = 8
COMPS = 3
KEYS = CORNERS * COMPS
BLOCK = 32
QUAD = 4
OPP = (1, 0, 3, 2, 5, 4)


def nt_dot(left, right):
    return lax.dot_general(left, right, (((1,), (1,)), ((), ())), preferred_element_type=F32)


def split(value, parts):
    out = []
    for _ in range(parts):
        head = value.astype(BF16)
        out.append(head)
        value = value - head.astype(F32)
    return out


def kernel(
    nx, ny,
    traces, visc_in, partner_in, owner_in, self_in, opp_in, cross_in, cmap_in,
    applied, coarse,
    raw, s_mat, o_mat, c_mat, cmap, visc, partner, owner,
    own, out1, in1, jump, w_s, w_o, w_c, local, in2,
    w_hi, w_lo, y_all, y_out, y_in, dense, z_in, quad_out, quad_in,
    load_sem, send1, recv1, send2, recv2, send_y, recv_y, send_z, recv_z, send_q, recv_q, far_sem,
):
    width = raw.shape[-1]
    nz = ny // QUAD
    reach = nz // 4
    sx, sy = lax.axis_index("sx"), lax.axis_index("sy")
    z, quad = sy // QUAD, lax.rem(sy, QUAD)

    def in_row(to):
        return (sx, lax.rem(to + ny, ny))

    beside = (
        (lax.rem(sx + 1, nx), sy),
        (lax.rem(sx + nx - 1, nx), sy),
        in_row(sy + 1),
        in_row(sy - 1),
    )
    inside = (sx < nx - 1, sx > 0, sy < ny - 1, sy > 0)
    quads = [(sx, z * QUAD + lax.rem(quad + j, QUAD)) for j in range(1, QUAD)]
    near = [in_row(sy + QUAD * d) for d in range(1, reach + 1)]
    near += [in_row(sy - QUAD * d) for d in range(1, reach + 1)]

    barrier = pltpu.get_barrier_semaphore()
    greeted = [*beside, *quads, *near]
    for device in greeted:
        pl.semaphore_signal(barrier, inc=1, device_id=device, device_id_type=MESH)

    loads = {}
    for i, (name, source, target) in enumerate((
        ("raw", traces.at[0, 0], raw),
        ("cmap", cmap_in, cmap),
        ("cross", cross_in, c_mat),
        ("self", self_in, s_mat),
        ("opp", opp_in, o_mat),
        ("visc", visc_in.at[0, 0], visc),
        ("partner", partner_in.at[0, 0], partner),
        ("owner", owner_in.at[0, 0], owner),
    )):
        loads[name] = pltpu.make_async_copy(source, target, load_sem.at[i])
        loads[name].start()

    def exchange(source, target, sends, recvs, f):
        copy = pltpu.make_async_remote_copy(
            src_ref=source,
            dst_ref=target.at[OPP[f]],
            send_sem=sends.at[f],
            recv_sem=recvs.at[OPP[f]],
            device_id=beside[f],
            device_id_type=MESH,
        )
        copy.start()
        return copy

    with jax.named_scope("repack"):
        loads["raw"].wait()
        for f in range(6):
            for s in range(SUBS):
                both = raw[s, f].astype(F32)
                for c in range(2):
                    own[c, f, s] = both[c * HALF : (c + 1) * HALF]
            if f < 4:
                for c in range(2):
                    out1[c, f] = own[c, f].reshape(SUBS * HALF, width).astype(BF16)

    with jax.named_scope("entry"):
        pl.semaphore_wait(barrier, len(greeted))

    copies1 = [[exchange(out1.at[0, f], in1.at[0], send1.at[0], recv1.at[0], f) for f in range(4)]]
    for device in (in_row(sy + QUAD * reach), in_row(sy - QUAD * reach)):
        pl.semaphore_signal(far_sem, inc=1, device_id=device, device_id_type=MESH)

    lane = lax.broadcasted_iota(jnp.int32, (1, 128), 1)
    block = lane // BLOCK

    def moved(value, shift):
        shift = (shift * BLOCK) % 128
        return pltpu.roll(value, shift, 1) if shift else value

    with jax.named_scope("weights"):
        loads["cmap"].wait()
        pad = jnp.zeros((BLOCK - KEYS, width), F32)
        faces = [jnp.concatenate([cmap[f].astype(F32), pad], 0) for f in range(6)]
        pairs = [faces[0] + faces[1], faces[2] + faces[3], faces[4] + faces[5]]
        adjacent = [pairs[1] + pairs[2], pairs[0] + pairs[2], pairs[0] + pairs[1]]
        adjacent = jnp.concatenate([adjacent[f // 2] for f in range(6)], 0)
        adj_hi, adj_lo = split(adjacent, 2)
        straight = jnp.concatenate(faces, 0).astype(BF16)
        flipped = jnp.concatenate([faces[OPP[f]] for f in range(6)], 0).astype(BF16)
        loads["cross"].wait()
        weight = nt_dot(adj_hi, c_mat[...]) + nt_dot(adj_lo, c_mat[...])
        loads["self"].wait()
        weight += nt_dot(straight, s_mat[...])
        loads["opp"].wait()
        weight += nt_dot(flipped, o_mat[...])
        w_hi[...], w_lo[...] = split(weight, 2)

    with jax.named_scope("corner_values"):
        flat = raw[...].reshape(SUBS * 6 * RHS, width)
        both = nt_dot(flat, w_hi[...]) + nt_dot(flat, w_lo[...])
        y_all[...] = both.reshape(SUBS, 6, RHS, 6 * BLOCK)

        def value_of(s, f, face, to):
            if face < 4:
                tile, at = y_all[s, f, :, :128], face
            else:
                tile = y_all[s, f, :, 128:]
                tile = jnp.concatenate([tile, jnp.zeros((RHS, 64), F32)], 1)
                at = face - 4
            return jnp.where(block == to, moved(tile, to - at), 0.0)

        copies_y = []
        for f in range(4):
            y_out[f] = sum(value_of(s, f, OPP[f], s) for s in range(SUBS))
            copies_y.append(exchange(y_out.at[f], y_in, send_y, recv_y, f))

    copies1.append([exchange(out1.at[1, f], in1.at[1], send1.at[1], recv1.at[1], f) for f in range(4)])

    with jax.named_scope("own_corners"):
        for name in ("visc", "partner", "owner"):
            loads[name].wait()
        parts = jnp.zeros((RHS, 128), F32)
        for s in range(SUBS):
            for f in range(6):
                parts += value_of(s, f, f, s)
            if s < SUBS - 1:
                parts -= value_of(s + 1, 5, 4, s)
            if s > 0:
                parts -= value_of(s - 1, 4, 5, s)
        visc_lanes = jnp.zeros((1, 128), F32)
        for s in range(SUBS):
            visc_lanes = jnp.where(block == s, visc[s], visc_lanes)
        row = lax.broadcasted_iota(jnp.int32, (SUBS * BLOCK, 1), 0)
        owners = jnp.full((SUBS * BLOCK, 1), -1, jnp.int32)
        for s in range(SUBS):
            for m in range(CORNERS):
                first = s * BLOCK + m * COMPS
                owners = jnp.where((row >= first) & (row < first + COMPS), owner[s, m], owners)
        unknown = lax.broadcasted_iota(jnp.int32, (SUBS * BLOCK, 8 * ny), 1)
        onehot = jnp.where(unknown == owners, 1.0, 0.0).astype(BF16)

    with jax.named_scope("corners"):
        for f in range(4):
            copies_y[f].wait_recv()
        for f in range(4):
            received = y_in[f]
            slots = jnp.zeros((1, 128), jnp.int32)
            for s in range(SUBS):
                slots = jnp.where(block == s, partner[s, f], slots)
            chosen = jnp.zeros((RHS, 128), F32)
            for d in range(SUBS):
                here = slots == lax.rem(block - d + SUBS, SUBS)
                chosen += jnp.where(here, moved(received, d), 0.0)
            parts -= jnp.where(inside[f], chosen, 0.0)
        parts = parts * visc_lanes
        comp = lax.rem(lax.rem(lane, BLOCK), COMPS)
        stacked = jnp.concatenate([jnp.where(comp == c, parts, 0.0) for c in range(COMPS)], 0)
        rows = COMPS * RHS
        total = jnp.dot(
            jnp.concatenate(split(stacked, 3), 0), onehot, preferred_element_type=F32
        )
        total = total[:rows] + total[rows : 2 * rows] + total[2 * rows :]
        for to in range(nz):
            tiles = total[:, to // 4 * 128 : to // 4 * 128 + 128]
            halves = []
            for groups in ((0, 1, 2, 3), (4, 5)):
                half = jnp.zeros((8, 128), F32)
                for g in groups:
                    value = moved(tiles[g * 8 : g * 8 + 8], g % 4 - to % 4)
                    half = jnp.where(block == g % 4, value, half)
                halves.append(half)
            dense[to] = jnp.concatenate(halves, 0)

    with jax.named_scope("corner_send"):
        pl.semaphore_wait(far_sem, 2)
        order = sorted(range(1, nz), key=lambda d: -min(d, nz - d))
        copies_z = {}
        for d in order:
            copies_z[d] = pltpu.make_async_remote_copy(
                src_ref=dense.at[lax.rem(z + d, nz)],
                dst_ref=z_in.at[d],
                send_sem=send_z.at[d],
                recv_sem=recv_z.at[d],
                device_id=in_row(sy + QUAD * d),
                device_id_type=MESH,
            )
            copies_z[d].start()

    def selected(f, received):
        received = received.astype(F32)
        slots = [received[p * HALF : (p + 1) * HALF] for p in range(SUBS)]
        values = []
        for s in range(SUBS):
            value = slots[0]
            for p in range(1, SUBS):
                value = jnp.where(partner[s, f] == p, slots[p], value)
            values.append(value)
        values = jnp.concatenate(values, 0)
        return jnp.where(inside[f], values, 0.0)

    none = jnp.zeros((HALF, width), F32)
    visc_rows = jnp.concatenate([jnp.full((HALF, width), visc[s], F32) for s in range(SUBS)], 0)
    size = SUBS * HALF

    copies2 = []
    for c in range(2):
        with jax.named_scope(f"wait_traces{c}"):
            for f in range(4):
                copies1[c][f].wait_recv()
        with jax.named_scope(f"local{c}"):
            for f in range(4):
                mine = own[c, f].reshape(size, width)
                jump[f * size : (f + 1) * size] = (mine - selected(f, in1[c, f])).astype(BF16)
            top, bottom = own[c, 4].reshape(size, width), own[c, 5].reshape(size, width)
            above = jnp.concatenate([bottom[HALF:], none], 0)
            below = jnp.concatenate([none, top[:-HALF]], 0)
            jump[4 * size : 5 * size] = (top - above).astype(BF16)
            jump[5 * size : 6 * size] = (bottom - below).astype(BF16)
            w_c[...] = jnp.dot(jump[...], c_mat[...], preferred_element_type=F32)
            w_s[...] = jnp.dot(jump[...], s_mat[...], preferred_element_type=F32)
            w_o[...] = jnp.dot(jump[...], o_mat[...], preferred_element_type=F32)

            def face(ref, f):
                return ref[f * size : (f + 1) * size]

            copies2.append([])
            for f in range(6):
                others = [g for g in range(6) if g // 2 != f // 2]
                value = face(w_s, f) + face(w_o, OPP[f])
                value += (face(w_c, others[0]) + face(w_c, others[1])) + (
                    face(w_c, others[2]) + face(w_c, others[3])
                )
                local[c, f] = (visc_rows * value).astype(BF16)
                if f < 4:
                    copies2[c].append(exchange(local.at[c, f], in2.at[c], send2.at[c], recv2.at[c], f))
            top, bottom = local[c, 4].astype(F32), local[c, 5].astype(F32)
            above = jnp.concatenate([bottom[HALF:], none], 0)
            below = jnp.concatenate([none, top[:-HALF]], 0)
            for f, value in ((4, top - above), (5, bottom - below)):
                for s in range(SUBS):
                    applied[0, 0, s, f, c * HALF : (c + 1) * HALF] = value[s * HALF : (s + 1) * HALF]

    def finish(c):
        with jax.named_scope(f"wait_local{c}"):
            for f in range(4):
                copies2[c][f].wait_recv()
        with jax.named_scope(f"applied{c}"):
            for f in range(4):
                value = local[c, f].astype(F32) - selected(f, in2[c, f])
                for s in range(SUBS):
                    applied[0, 0, s, f, c * HALF : (c + 1) * HALF] = value[s * HALF : (s + 1) * HALF]

    with jax.named_scope("corner_sum"):
        for d in range(1, nz):
            copies_z[d].wait_recv()
        values = [dense[z]] + [z_in[d] for d in range(1, nz)]
        while len(values) > 1:
            values = [a + b for a, b in zip(values[::2], values[1::2])] + values[len(values) & ~1 :]
        quad_out[...] = values[0]
        copies_q = []
        for j in range(1, QUAD):
            copies_q.append(pltpu.make_async_remote_copy(
                src_ref=quad_out,
                dst_ref=quad_in.at[j],
                send_sem=send_q.at[j],
                recv_sem=recv_q.at[j],
                device_id=quads[j - 1],
                device_id_type=MESH,
            ))
            copies_q[-1].start()

    finish(0)

    with jax.named_scope("corner_end"):
        for copy in copies_q:
            copy.wait_recv()
        result = (quad_out[...] + quad_in[1]) + (quad_in[2] + quad_in[3])
        mine = result
        for j in range(1, QUAD):
            mine = jnp.where(quad == j, pltpu.roll(result, 128 - 8 * j, 1), mine)
        for g in range(6):
            value = moved(mine[g // 4 * 8 : g // 4 * 8 + 8], -(g % 4))
            coarse[pl.ds(g % 2 * HALF * COMPS + g // 2, HALF, stride=COMPS)] = value

    finish(1)

    with jax.named_scope("sent"):
        for copy in [*copies1[0], *copies1[1], *copies_y, *copies_z.values(), *copies_q, *copies2[0], *copies2[1]]:
            copy.wait_send()


def body(traces, viscosity, partner, corner_owner, self_block, opposite_block, cross_block, corner_map):
    nx, ny = lax.axis_size("sx"), lax.axis_size("sy")
    width = traces.shape[-1]
    nz = ny // QUAD
    vmem, dma = pltpu.VMEM, pltpu.SemaphoreType.DMA
    size = SUBS * HALF
    applied, coarse = pl.pallas_call(
        functools.partial(kernel, nx, ny),
        out_shape=(
            jax.ShapeDtypeStruct(traces.shape, F32),
            jax.ShapeDtypeStruct((RHS * COMPS, 128), F32),
        ),
        in_specs=[pl.BlockSpec(memory_space=pltpu.HBM)] * 8,
        out_specs=(pl.BlockSpec(memory_space=vmem), pl.BlockSpec(memory_space=vmem)),
        scratch_shapes=[
            vmem((SUBS, 6, RHS, width), BF16),
            vmem((width, width), BF16),
            vmem((width, width), BF16),
            vmem((width, width), BF16),
            vmem((6, KEYS, width), BF16),
            pltpu.SMEM((SUBS,), F32),
            pltpu.SMEM((SUBS, 4), jnp.int32),
            pltpu.SMEM((SUBS, CORNERS), jnp.int32),
            vmem((2, 6, SUBS, HALF, width), F32),
            vmem((2, 4, size, width), BF16),
            vmem((2, 4, size, width), BF16),
            vmem((6 * size, width), BF16),
            vmem((6 * size, width), F32),
            vmem((6 * size, width), F32),
            vmem((6 * size, width), F32),
            vmem((2, 6, size, width), BF16),
            vmem((2, 4, size, width), BF16),
            vmem((6 * BLOCK, width), BF16),
            vmem((6 * BLOCK, width), BF16),
            vmem((SUBS, 6, RHS, 6 * BLOCK), F32),
            vmem((4, RHS, 128), F32),
            vmem((4, RHS, 128), F32),
            vmem((nz, 16, 128), F32),
            vmem((nz, 16, 128), F32),
            vmem((16, 128), F32),
            vmem((QUAD, 16, 128), F32),
            dma((8,)),
            dma((2, 4)),
            dma((2, 4)),
            dma((2, 4)),
            dma((2, 4)),
            dma((4,)),
            dma((4,)),
            dma((nz,)),
            dma((nz,)),
            dma((QUAD,)),
            dma((QUAD,)),
            pltpu.SemaphoreType.REGULAR,
        ],
        compiler_params=pltpu.CompilerParams(
            collective_id=0, has_side_effects=True, vmem_limit_bytes=40 * 2**20
        ),
    )(traces, viscosity, partner, corner_owner, self_block, opposite_block, cross_block, jnp.transpose(corner_map, (1, 0, 2)))
    return applied, coarse[:, :8]


def solution(mesh):
    return jax.shard_map(
        body,
        mesh=mesh,
        in_specs=(
            P("sx", "sy", None, None, None, None),
            P("sx", "sy", None),
            P("sx", "sy", None, None),
            P("sx", "sy", None, None),
            P(),
            P(),
            P(),
            P(),
        ),
        out_specs=(P("sx", "sy", None, None, None, None), P(None, ("sx", "sy"))),
        check_vma=False,
    )
```

```python
import functools

import jax
import jax.numpy as jnp
from jax import lax
from jax.experimental import pallas as pl
from jax.experimental.pallas import tpu as pltpu
from jax.sharding import PartitionSpec as P

MESH = pl.DeviceIdType.MESH
F32, BF16 = jnp.float32, jnp.bfloat16
SUBS = 4
RHS = 16
HALF = 8
CORNERS = 8
COMPS = 3
KEYS = CORNERS * COMPS
BLOCK = 32
QUAD = 4
OPP = (1, 0, 3, 2, 5, 4)


def nt_dot(left, right):
    return lax.dot_general(left, right, (((1,), (1,)), ((), ())), preferred_element_type=F32)


def split(value, parts):
    out = []
    for _ in range(parts):
        head = value.astype(BF16)
        out.append(head)
        value = value - head.astype(F32)
    return out


def kernel(
    nx, ny,
    traces, visc_in, partner_in, owner_in, self_in, opp_in, cross_in, cmap_in,
    applied, coarse,
    raw, s_mat, o_mat, c_mat, cmap, visc, partner, owner,
    own, out1, in1, jump, w_s, w_o, w_c, local, in2,
    w_hi, w_lo, dense, z_in, quad_out, quad_in,
    load_sem, send1, recv1, send2, recv2, send_z, recv_z, send_q, recv_q, far_sem,
):
    width = raw.shape[-1]
    nz = ny // QUAD
    reach = nz // 4
    sx, sy = lax.axis_index("sx"), lax.axis_index("sy")
    z, quad = sy // QUAD, lax.rem(sy, QUAD)

    def in_row(to):
        return (sx, lax.rem(to + ny, ny))

    beside = (
        (lax.rem(sx + 1, nx), sy),
        (lax.rem(sx + nx - 1, nx), sy),
        in_row(sy + 1),
        in_row(sy - 1),
    )
    inside = (sx < nx - 1, sx > 0, sy < ny - 1, sy > 0)
    quads = [(sx, z * QUAD + lax.rem(quad + j, QUAD)) for j in range(1, QUAD)]
    near = [in_row(sy + QUAD * d) for d in range(1, reach + 1)]
    near += [in_row(sy - QUAD * d) for d in range(1, reach + 1)]

    barrier = pltpu.get_barrier_semaphore()
    greeted = [*beside, *quads, *near]
    with jax.named_scope("greet"):
        for device in greeted:
            pl.semaphore_signal(barrier, inc=1, device_id=device, device_id_type=MESH)

    loads = {}
    for i, (name, source, target) in enumerate((
        ("raw", traces.at[0, 0], raw),
        ("cmap", cmap_in, cmap),
        ("cross", cross_in, c_mat),
        ("self", self_in, s_mat),
        ("opp", opp_in, o_mat),
        ("visc", visc_in.at[0, 0], visc),
        ("partner", partner_in.at[0, 0], partner),
        ("owner", owner_in.at[0, 0], owner),
    )):
        loads[name] = pltpu.make_async_copy(source, target, load_sem.at[i])
        loads[name].start()

    def exchange(source, target, sends, recvs, f):
        copy = pltpu.make_async_remote_copy(
            src_ref=source,
            dst_ref=target.at[OPP[f]],
            send_sem=sends.at[f],
            recv_sem=recvs.at[OPP[f]],
            device_id=beside[f],
            device_id_type=MESH,
        )
        copy.start()
        return copy

    with jax.named_scope("repack"):
        loads["raw"].wait()
        for f in range(6):
            for s in range(SUBS):
                both = raw[s, f].astype(F32)
                for c in range(2):
                    own[c, f, s] = both[c * HALF : (c + 1) * HALF]
            if f < 4:
                for c in range(2):
                    out1[c, f] = own[c, f].reshape(SUBS * HALF, width).astype(BF16)

    with jax.named_scope("entry"):
        pl.semaphore_wait(barrier, len(greeted))

    copies1 = [
        [exchange(out1.at[c, f], in1.at[c], send1.at[c], recv1.at[c], f) for f in range(4)]
        for c in range(2)
    ]
    for device in (in_row(sy + QUAD * reach), in_row(sy - QUAD * reach)):
        pl.semaphore_signal(far_sem, inc=1, device_id=device, device_id_type=MESH)

    lane = lax.broadcasted_iota(jnp.int32, (1, 128), 1)
    block = lane // BLOCK

    def moved(value, shift):
        shift = (shift * BLOCK) % 128
        return pltpu.roll(value, shift, 1) if shift else value

    with jax.named_scope("weights"):
        loads["cmap"].wait()
        pad = jnp.zeros((BLOCK - KEYS, width), F32)
        faces = [jnp.concatenate([cmap[f].astype(F32), pad], 0) for f in range(6)]
        pairs = [faces[0] + faces[1], faces[2] + faces[3], faces[4] + faces[5]]
        adjacent = [pairs[1] + pairs[2], pairs[0] + pairs[2], pairs[0] + pairs[1]]
        adjacent = jnp.concatenate([adjacent[f // 2] for f in range(6)], 0)
        adj_hi, adj_lo = split(adjacent, 2)
        straight = jnp.concatenate(faces, 0).astype(BF16)
        flipped = jnp.concatenate([faces[OPP[f]] for f in range(6)], 0).astype(BF16)
        loads["cross"].wait()
        weight = nt_dot(adj_hi, c_mat[...]) + nt_dot(adj_lo, c_mat[...])
        loads["self"].wait()
        weight += nt_dot(straight, s_mat[...])
        loads["opp"].wait()
        weight += nt_dot(flipped, o_mat[...])
        rest = jnp.zeros((2 * BLOCK, width), F32)
        w_hi[...], w_lo[...] = split(jnp.concatenate([weight, rest], 0), 2)

    with jax.named_scope("owners"):
        for name in ("visc", "partner", "owner"):
            loads[name].wait()
        visc_lanes = jnp.zeros((1, 128), F32)
        for s in range(SUBS):
            visc_lanes = jnp.where(block == s, visc[s], visc_lanes)
        row = lax.broadcasted_iota(jnp.int32, (SUBS * BLOCK, 1), 0)
        owners = jnp.full((SUBS * BLOCK, 1), -1, jnp.int32)
        for s in range(SUBS):
            for m in range(CORNERS):
                first = s * BLOCK + m * COMPS
                owners = jnp.where((row >= first) & (row < first + COMPS), owner[s, m], owners)
        unknown = lax.broadcasted_iota(jnp.int32, (SUBS * BLOCK, 8 * ny), 1)
        onehot = jnp.where(unknown == owners, 1.0, 0.0).astype(BF16)

    def selected(f, received):
        received = received.astype(F32)
        slots = [received[p * HALF : (p + 1) * HALF] for p in range(SUBS)]
        values = []
        for s in range(SUBS):
            value = slots[0]
            for p in range(1, SUBS):
                value = jnp.where(partner[s, f] == p, slots[p], value)
            values.append(value)
        values = jnp.concatenate(values, 0)
        return jnp.where(inside[f], values, 0.0)

    none = jnp.zeros((HALF, width), F32)
    visc_rows = jnp.concatenate([jnp.full((HALF, width), visc[s], F32) for s in range(SUBS)], 0)
    size = SUBS * HALF

    def corner_values(pairs):
        values = jnp.zeros((HALF, 128), F32)
        for s in range(SUBS):
            rows = [pairs[f * size + s * HALF : f * size + (s + 1) * HALF] for f in range(6)]
            tiles = [rows[f][:, f // 4 * 128 : f // 4 * 128 + 128] for f in range(6)]
            tiles = [tiles[0] + tiles[4], tiles[1] + tiles[5], tiles[2], tiles[3]]
            for f in range(4):
                values += jnp.where(block == s, moved(tiles[f], s - f), 0.0)
        return values * visc_lanes

    def send_corners(parts):
        comp = lax.rem(lax.rem(lane, BLOCK), COMPS)
        stacked = jnp.concatenate([jnp.where(comp == c, parts, 0.0) for c in range(COMPS)], 0)
        rows = COMPS * RHS
        total = jnp.dot(
            jnp.concatenate(split(stacked, 3), 0), onehot, preferred_element_type=F32
        )
        total = total[:rows] + total[rows : 2 * rows] + total[2 * rows :]
        for to in range(nz):
            tiles = total[:, to // 4 * 128 : to // 4 * 128 + 128]
            halves = []
            for groups in ((0, 1, 2, 3), (4, 5)):
                half = jnp.zeros((8, 128), F32)
                for g in groups:
                    value = moved(tiles[g * 8 : g * 8 + 8], g % 4 - to % 4)
                    half = jnp.where(block == g % 4, value, half)
                halves.append(half)
            dense[to] = jnp.concatenate(halves, 0)

        pl.semaphore_wait(far_sem, 2)
        order = sorted(range(1, nz), key=lambda d: -min(d, nz - d))
        copies_z = {}
        for d in order:
            copies_z[d] = pltpu.make_async_remote_copy(
                src_ref=dense.at[lax.rem(z + d, nz)],
                dst_ref=z_in.at[d],
                send_sem=send_z.at[d],
                recv_sem=recv_z.at[d],
                device_id=in_row(sy + QUAD * d),
                device_id_type=MESH,
            )
            copies_z[d].start()
        return copies_z

    copies2, corner_parts = [], []
    for c in range(2):
        with jax.named_scope(f"wait_traces{c}"):
            for f in range(4):
                copies1[c][f].wait_recv()
        with jax.named_scope(f"local{c}"):
            for f in range(4):
                mine = own[c, f].reshape(size, width)
                jump[f * size : (f + 1) * size] = (mine - selected(f, in1[c, f])).astype(BF16)
            top, bottom = own[c, 4].reshape(size, width), own[c, 5].reshape(size, width)
            above = jnp.concatenate([bottom[HALF:], none], 0)
            below = jnp.concatenate([none, top[:-HALF]], 0)
            jump[4 * size : 5 * size] = (top - above).astype(BF16)
            jump[5 * size : 6 * size] = (bottom - below).astype(BF16)
            pairs = nt_dot(jump[...], w_hi[...]) + nt_dot(jump[...], w_lo[...])
            corner_parts.append(corner_values(pairs))
            if c == 1:
                with jax.named_scope("corners"):
                    copies_z = send_corners(jnp.concatenate(corner_parts, 0))
            w_c[...] = jnp.dot(jump[...], c_mat[...], preferred_element_type=F32)
            w_s[...] = jnp.dot(jump[...], s_mat[...], preferred_element_type=F32)
            w_o[...] = jnp.dot(jump[...], o_mat[...], preferred_element_type=F32)

            def face(ref, f):
                return ref[f * size : (f + 1) * size]

            copies2.append([])
            for f in range(6):
                others = [g for g in range(6) if g // 2 != f // 2]
                value = face(w_s, f) + face(w_o, OPP[f])
                value += (face(w_c, others[0]) + face(w_c, others[1])) + (
                    face(w_c, others[2]) + face(w_c, others[3])
                )
                local[c, f] = (visc_rows * value).astype(BF16)
                if f < 4:
                    copies2[c].append(exchange(local.at[c, f], in2.at[c], send2.at[c], recv2.at[c], f))
            top, bottom = local[c, 4].astype(F32), local[c, 5].astype(F32)
            above = jnp.concatenate([bottom[HALF:], none], 0)
            below = jnp.concatenate([none, top[:-HALF]], 0)
            for f, value in ((4, top - above), (5, bottom - below)):
                for s in range(SUBS):
                    applied[0, 0, s, f, c * HALF : (c + 1) * HALF] = value[s * HALF : (s + 1) * HALF]

    def finish(c):
        with jax.named_scope(f"wait_local{c}"):
            for f in range(4):
                copies2[c][f].wait_recv()
        with jax.named_scope(f"applied{c}"):
            for f in range(4):
                value = local[c, f].astype(F32) - selected(f, in2[c, f])
                for s in range(SUBS):
                    applied[0, 0, s, f, c * HALF : (c + 1) * HALF] = value[s * HALF : (s + 1) * HALF]

    with jax.named_scope("corner_sum"):
        for d in range(1, nz):
            copies_z[d].wait_recv()
        values = [dense[z]] + [z_in[d] for d in range(1, nz)]
        while len(values) > 1:
            values = [a + b for a, b in zip(values[::2], values[1::2])] + values[len(values) & ~1 :]
        quad_out[...] = values[0]
        copies_q = []
        for j in range(1, QUAD):
            copies_q.append(pltpu.make_async_remote_copy(
                src_ref=quad_out,
                dst_ref=quad_in.at[j],
                send_sem=send_q.at[j],
                recv_sem=recv_q.at[j],
                device_id=quads[j - 1],
                device_id_type=MESH,
            ))
            copies_q[-1].start()

    finish(0)

    with jax.named_scope("corner_end"):
        for copy in copies_q:
            copy.wait_recv()
        result = (quad_out[...] + quad_in[1]) + (quad_in[2] + quad_in[3])
        mine = result
        for j in range(1, QUAD):
            mine = jnp.where(quad == j, pltpu.roll(result, 128 - 8 * j, 1), mine)
        for g in range(6):
            value = moved(mine[g // 4 * 8 : g // 4 * 8 + 8], -(g % 4))
            coarse[pl.ds(g % 2 * HALF * COMPS + g // 2, HALF, stride=COMPS)] = value

    finish(1)

    with jax.named_scope("sent"):
        for copy in [*copies1[0], *copies1[1], *copies_z.values(), *copies_q, *copies2[0], *copies2[1]]:
            copy.wait_send()


def body(traces, viscosity, partner, corner_owner, self_block, opposite_block, cross_block, corner_map):
    nx, ny = lax.axis_size("sx"), lax.axis_size("sy")
    width = traces.shape[-1]
    nz = ny // QUAD
    vmem, dma = pltpu.VMEM, pltpu.SemaphoreType.DMA
    size = SUBS * HALF
    inputs = (
        traces, viscosity, partner, corner_owner, self_block, opposite_block, cross_block,
        jnp.transpose(corner_map, (1, 0, 2)),
    )
    inputs = [pltpu.with_memory_space_constraint(value, pltpu.HBM) for value in inputs]
    applied, coarse = pl.pallas_call(
        functools.partial(kernel, nx, ny),
        out_shape=(
            jax.ShapeDtypeStruct(traces.shape, F32),
            jax.ShapeDtypeStruct((RHS * COMPS, 128), F32),
        ),
        in_specs=[pl.BlockSpec(memory_space=pltpu.HBM)] * 8,
        out_specs=(pl.BlockSpec(memory_space=vmem), pl.BlockSpec(memory_space=vmem)),
        scratch_shapes=[
            vmem((SUBS, 6, RHS, width), BF16),
            vmem((width, width), BF16),
            vmem((width, width), BF16),
            vmem((width, width), BF16),
            vmem((6, KEYS, width), BF16),
            pltpu.SMEM((SUBS,), F32),
            pltpu.SMEM((SUBS, 4), jnp.int32),
            pltpu.SMEM((SUBS, CORNERS), jnp.int32),
            vmem((2, 6, SUBS, HALF, width), F32),
            vmem((2, 4, size, width), BF16),
            vmem((2, 4, size, width), BF16),
            vmem((6 * size, width), BF16),
            vmem((6 * size, width), F32),
            vmem((6 * size, width), F32),
            vmem((6 * size, width), F32),
            vmem((2, 6, size, width), BF16),
            vmem((2, 4, size, width), BF16),
            vmem((8 * BLOCK, width), BF16),
            vmem((8 * BLOCK, width), BF16),
            vmem((nz, 16, 128), F32),
            vmem((nz, 16, 128), F32),
            vmem((16, 128), F32),
            vmem((QUAD, 16, 128), F32),
            dma((8,)),
            dma((2, 4)),
            dma((2, 4)),
            dma((2, 4)),
            dma((2, 4)),
            dma((nz,)),
            dma((nz,)),
            dma((QUAD,)),
            dma((QUAD,)),
            pltpu.SemaphoreType.REGULAR,
        ],
        compiler_params=pltpu.CompilerParams(
            collective_id=0, has_side_effects=True, vmem_limit_bytes=40 * 2**20
        ),
    )(*inputs)
    return applied, coarse[:, :8]


def solution(mesh):
    return jax.shard_map(
        body,
        mesh=mesh,
        in_specs=(
            P("sx", "sy", None, None, None, None),
            P("sx", "sy", None),
            P("sx", "sy", None, None),
            P("sx", "sy", None, None),
            P(),
            P(),
            P(),
            P(),
        ),
        out_specs=(P("sx", "sy", None, None, None, None), P(None, ("sx", "sy"))),
        check_vma=False,
    )
```

```python
import functools

import jax
import jax.numpy as jnp
from jax import lax
from jax.experimental import pallas as pl
from jax.experimental.pallas import tpu as pltpu
from jax.sharding import PartitionSpec as P

MESH = pl.DeviceIdType.MESH
F32, BF16 = jnp.float32, jnp.bfloat16
SUBS = 4
RHS = 16
HALF = 8
CORNERS = 8
COMPS = 3
KEYS = CORNERS * COMPS
BLOCK = 32
QUAD = 4
OPP = (1, 0, 3, 2, 5, 4)


def nt_dot(left, right):
    return lax.dot_general(left, right, (((1,), (1,)), ((), ())), preferred_element_type=F32)


def split(value, parts):
    out = []
    for _ in range(parts):
        head = value.astype(BF16)
        out.append(head)
        value = value - head.astype(F32)
    return out


def kernel(
    nx, ny,
    traces, visc_in, partner_in, owner_in, self_in, opp_in, cross_in, cmap_in,
    applied, coarse,
    raw, s_mat, o_mat, c_mat, cmap, visc, partner, owner,
    own, out1, in1, jump, w_s, w_o, w_c, local, in2,
    w_hi, w_lo, y_all, y_out, y_in, dense, z_in, quad_out, quad_in,
    load_sem, send1, recv1, send2, recv2, send_y, recv_y, send_z, recv_z, send_q, recv_q, far_sem,
):
    width = raw.shape[-1]
    nz = ny // QUAD
    sx, sy = lax.axis_index("sx"), lax.axis_index("sy")
    z, quad = sy // QUAD, lax.rem(sy, QUAD)

    def in_row(to):
        return (sx, lax.rem(to + ny, ny))

    beside = (
        (lax.rem(sx + 1, nx), sy),
        (lax.rem(sx + nx - 1, nx), sy),
        in_row(sy + 1),
        in_row(sy - 1),
    )
    inside = (sx < nx - 1, sx > 0, sy < ny - 1, sy > 0)
    quads = [(sx, z * QUAD + lax.rem(quad + j, QUAD)) for j in range(1, QUAD)]

    barrier = pltpu.get_barrier_semaphore()

    def signal(semaphore, device):
        pl.semaphore_signal(semaphore, inc=1, device_id=device, device_id_type=MESH)

    with jax.named_scope("greet"):
        for f in range(4):
            pl.when(inside[f])(functools.partial(signal, barrier, beside[f]))
        for device in quads:
            signal(barrier, device)
        for d in range(1, nz):
            pl.when(z + d < nz)(functools.partial(signal, barrier, in_row(sy + QUAD * d)))

    loads = {}
    for i, (name, source, target) in enumerate((
        ("raw", traces.at[0, 0], raw),
        ("cmap", cmap_in, cmap),
        ("cross", cross_in, c_mat),
        ("self", self_in, s_mat),
        ("opp", opp_in, o_mat),
        ("visc", visc_in.at[0, 0], visc),
        ("partner", partner_in.at[0, 0], partner),
        ("owner", owner_in.at[0, 0], owner),
    )):
        loads[name] = pltpu.make_async_copy(source, target, load_sem.at[i])
        loads[name].start()

    def exchange(source, target, sends, recvs, f):
        copy = pltpu.make_async_remote_copy(
            src_ref=source,
            dst_ref=target.at[OPP[f]],
            send_sem=sends.at[f],
            recv_sem=recvs.at[OPP[f]],
            device_id=beside[f],
            device_id_type=MESH,
        )
        pl.when(inside[f])(copy.start)
        return (
            lambda: pl.when(inside[OPP[f]])(copy.wait_recv),
            lambda: pl.when(inside[f])(copy.wait_send),
        )

    lane = lax.broadcasted_iota(jnp.int32, (1, 128), 1)
    block = lane // BLOCK

    def moved(value, shift):
        shift = (shift * BLOCK) % 128
        return pltpu.roll(value, shift, 1) if shift else value

    with jax.named_scope("weights"):
        loads["cmap"].wait()
        pad = jnp.zeros((BLOCK - KEYS, width), F32)
        faces = [jnp.concatenate([cmap[f].astype(F32), pad], 0) for f in range(6)]
        straight = jnp.concatenate(faces, 0).astype(BF16)
        products = []
        for name, matrix in (("cross", c_mat), ("self", s_mat), ("opp", o_mat)):
            loads[name].wait()
            product = nt_dot(straight, matrix[...])
            products.append([product[f * BLOCK : (f + 1) * BLOCK] for f in range(6)])
        cross, same, across = products
        pairs = [cross[0] + cross[1], cross[2] + cross[3], cross[4] + cross[5]]
        adjacent = [pairs[1] + pairs[2], pairs[0] + pairs[2], pairs[0] + pairs[1]]
        weight = [same[f] + across[OPP[f]] + adjacent[f // 2] for f in range(6)]
        weight.append(jnp.zeros((2 * BLOCK, width), F32))
        w_hi[...], w_lo[...] = split(jnp.concatenate(weight, 0), 2)

    def value_of(s, f, face, to):
        tile = y_all[s, f, :, face // 4 * 128 : face // 4 * 128 + 128]
        return jnp.where(block == to, moved(tile, to - face % 4), 0.0)

    with jax.named_scope("values"):
        loads["raw"].wait()
        flat = raw[...].reshape(SUBS * 6 * RHS, width)
        both = nt_dot(flat, w_hi[...]) + nt_dot(flat, w_lo[...])
        y_all[...] = both.reshape(SUBS, 6, RHS, 8 * BLOCK)
        for f in range(4):
            y_out[f] = sum(value_of(s, f, OPP[f], s) for s in range(SUBS))

    with jax.named_scope("entry"):
        pl.semaphore_wait(barrier, sum(here.astype(jnp.int32) for here in inside) + len(quads) + z)

    copies_y = [exchange(y_out.at[f], y_in, send_y, recv_y, f) for f in range(4)]
    for d in range(1, nz):
        pl.when(z >= d)(functools.partial(signal, far_sem, in_row(sy - QUAD * d)))

    with jax.named_scope("repack"):
        for f in range(6):
            for s in range(SUBS):
                both = raw[s, f].astype(F32)
                for c in range(2):
                    own[c, f, s] = both[c * HALF : (c + 1) * HALF]
            if f < 4:
                for c in range(2):
                    out1[c, f] = own[c, f].reshape(SUBS * HALF, width).astype(BF16)

    copies1 = [
        [exchange(out1.at[c, f], in1.at[c], send1.at[c], recv1.at[c], f) for f in range(4)]
        for c in range(2)
    ]

    for f in range(4):
        def clear(f=f):
            y_in[f] = jnp.zeros(y_in.shape[1:], F32)
            for ref in (in1, in2):
                for c in range(2):
                    ref[c, f] = jnp.zeros(ref.shape[2:], BF16)

        pl.when(jnp.logical_not(inside[f]))(clear)

    with jax.named_scope("owners"):
        for name in ("visc", "partner", "owner"):
            loads[name].wait()
        visc_lanes = jnp.zeros((1, 128), F32)
        for s in range(SUBS):
            visc_lanes = jnp.where(block == s, visc[s], visc_lanes)
        row = lax.broadcasted_iota(jnp.int32, (SUBS * BLOCK, 1), 0)
        owners = jnp.full((SUBS * BLOCK, 1), -1, jnp.int32)
        for s in range(SUBS):
            for m in range(CORNERS):
                first = s * BLOCK + m * COMPS
                owners = jnp.where((row >= first) & (row < first + COMPS), owner[s, m], owners)
        unknown = lax.broadcasted_iota(jnp.int32, (SUBS * BLOCK, 8 * ny), 1)
        onehot = jnp.where(unknown == owners, 1.0, 0.0).astype(BF16)
        parts = jnp.zeros((RHS, 128), F32)
        for s in range(SUBS):
            for f in range(6):
                parts += value_of(s, f, f, s)
            if s < SUBS - 1:
                parts -= value_of(s + 1, 5, 4, s)
            if s > 0:
                parts -= value_of(s - 1, 4, 5, s)

    with jax.named_scope("wait_values"):
        for wait, _ in copies_y:
            wait()

    with jax.named_scope("corners"):
        for f in range(4):
            received = y_in[f]
            slots = jnp.zeros((1, 128), jnp.int32)
            for s in range(SUBS):
                slots = jnp.where(block == s, partner[s, f], slots)
            for d in range(SUBS):
                here = slots == lax.rem(block - d + SUBS, SUBS)
                parts -= jnp.where(here, moved(received, d), 0.0)
        parts = parts * visc_lanes
        comp = lax.rem(lax.rem(lane, BLOCK), COMPS)
        stacked = jnp.concatenate([jnp.where(comp == c, parts, 0.0) for c in range(COMPS)], 0)
        rows = COMPS * RHS
        total = jnp.dot(
            jnp.concatenate(split(stacked, 3), 0), onehot, preferred_element_type=F32
        )
        total = total[:rows] + total[rows : 2 * rows] + total[2 * rows :]
        for to in range(nz):
            tiles = total[:, to // 4 * 128 : to // 4 * 128 + 128]
            halves = []
            for groups in ((0, 1, 2, 3), (4, 5)):
                half = jnp.zeros((8, 128), F32)
                for g in groups:
                    value = moved(tiles[g * 8 : g * 8 + 8], g % 4 - to % 4)
                    half = jnp.where(block == g % 4, value, half)
                halves.append(half)
            dense[to, :8] = halves[0]
            dense[to, 8:] = jnp.where(block < 2, halves[1][:4], moved(halves[1][4:], 2))

    order = sorted(range(1, nz), key=lambda d: -min(d, nz - d))
    copies_z = {}
    for d in order:
        copies_z[d] = pltpu.make_async_remote_copy(
            src_ref=dense.at[lax.rem(z + d, nz)],
            dst_ref=z_in.at[d],
            send_sem=send_z.at[d],
            recv_sem=recv_z.at[d],
            device_id=in_row(sy + QUAD * d),
            device_id_type=MESH,
        )
        pl.when(z + d >= nz)(copies_z[d].start)

    def selected(f, received):
        received = received.astype(F32)
        slots = [received[p * HALF : (p + 1) * HALF] for p in range(SUBS)]
        values = []
        for s in range(SUBS):
            value = slots[0]
            for p in range(1, SUBS):
                value = jnp.where(partner[s, f] == p, slots[p], value)
            values.append(value)
        return jnp.concatenate(values, 0)

    none = jnp.zeros((HALF, width), F32)
    visc_rows = jnp.concatenate([jnp.full((HALF, width), visc[s], F32) for s in range(SUBS)], 0)
    size = SUBS * HALF

    copies2 = []
    for c in range(2):
        with jax.named_scope(f"wait_traces{c}"):
            for wait, _ in copies1[c]:
                wait()
        with jax.named_scope(f"local{c}"):
            for f in range(4):
                mine = own[c, f].reshape(size, width)
                jump[f * size : (f + 1) * size] = (mine - selected(f, in1[c, f])).astype(BF16)
            top, bottom = own[c, 4].reshape(size, width), own[c, 5].reshape(size, width)
            above = jnp.concatenate([bottom[HALF:], none], 0)
            below = jnp.concatenate([none, top[:-HALF]], 0)
            jump[4 * size : 5 * size] = (top - above).astype(BF16)
            jump[5 * size : 6 * size] = (bottom - below).astype(BF16)
            w_c[...] = jnp.dot(jump[...], c_mat[...], preferred_element_type=F32)
            w_s[...] = jnp.dot(jump[...], s_mat[...], preferred_element_type=F32)
            w_o[...] = jnp.dot(jump[...], o_mat[...], preferred_element_type=F32)

            def face(ref, f):
                return ref[f * size : (f + 1) * size]

            copies2.append([])
            for f in range(6):
                others = [g for g in range(6) if g // 2 != f // 2]
                value = face(w_s, f) + face(w_o, OPP[f])
                value += (face(w_c, others[0]) + face(w_c, others[1])) + (
                    face(w_c, others[2]) + face(w_c, others[3])
                )
                local[c, f] = (visc_rows * value).astype(BF16)
                if f < 4:
                    copies2[c].append(exchange(local.at[c, f], in2.at[c], send2.at[c], recv2.at[c], f))
            top, bottom = local[c, 4].astype(F32), local[c, 5].astype(F32)
            above = jnp.concatenate([bottom[HALF:], none], 0)
            below = jnp.concatenate([none, top[:-HALF]], 0)
            for f, value in ((4, top - above), (5, bottom - below)):
                for s in range(SUBS):
                    applied[0, 0, s, f, c * HALF : (c + 1) * HALF] = value[s * HALF : (s + 1) * HALF]

    def finish(c):
        with jax.named_scope(f"wait_local{c}"):
            for wait, _ in copies2[c]:
                wait()
        with jax.named_scope(f"applied{c}"):
            for f in range(4):
                value = local[c, f].astype(F32) - selected(f, in2[c, f])
                for s in range(SUBS):
                    applied[0, 0, s, f, c * HALF : (c + 1) * HALF] = value[s * HALF : (s + 1) * HALF]

    with jax.named_scope("far"):
        pl.when(z < nz - 1)(lambda: pl.semaphore_wait(far_sem, nz - 1 - z))
        for d in order:
            pl.when(z + d < nz)(copies_z[d].start)

    finish(0)
    finish(1)

    with jax.named_scope("corner_sum"):
        mine = dense[0]
        for at in range(1, nz):
            mine = jnp.where(z == at, dense[at], mine)
        for d in range(1, nz):
            copies_z[d].wait_recv()
        values = [mine] + [z_in[d] for d in range(1, nz)]
        while len(values) > 1:
            values = [a + b for a, b in zip(values[::2], values[1::2])] + values[len(values) & ~1 :]
        quad_out[...] = values[0]
        copies_q = []
        for j in range(1, QUAD):
            copies_q.append(pltpu.make_async_remote_copy(
                src_ref=quad_out,
                dst_ref=quad_in.at[j],
                send_sem=send_q.at[j],
                recv_sem=recv_q.at[j],
                device_id=quads[j - 1],
                device_id_type=MESH,
            ))
            copies_q[-1].start()

    with jax.named_scope("corner_end"):
        for copy in copies_q:
            copy.wait_recv()
        result = (quad_out[...] + quad_in[1]) + (quad_in[2] + quad_in[3])
        mine = result
        for j in range(1, QUAD):
            mine = jnp.where(quad == j, pltpu.roll(result, 128 - 8 * j, 1), mine)
        low = mine[8:]
        tiles = (mine[:8], jnp.concatenate([low, moved(low, -2)], 0))
        for g in range(6):
            coarse[pl.ds(g % 2 * HALF * COMPS + g // 2, HALF, stride=COMPS)] = moved(tiles[g // 4], -(g % 4))

    with jax.named_scope("sent"):
        for copy in [*copies_z.values(), *copies_q]:
            copy.wait_send()
        for _, wait in [*copies_y, *copies1[0], *copies1[1], *copies2[0], *copies2[1]]:
            wait()


def body(traces, viscosity, partner, corner_owner, self_block, opposite_block, cross_block, corner_map):
    nx, ny = lax.axis_size("sx"), lax.axis_size("sy")
    width = traces.shape[-1]
    nz = ny // QUAD
    vmem, dma = pltpu.VMEM, pltpu.SemaphoreType.DMA
    size = SUBS * HALF
    inputs = (
        traces, viscosity, partner, corner_owner, self_block, opposite_block, cross_block,
        jnp.transpose(corner_map, (1, 0, 2)),
    )
    inputs = [pltpu.with_memory_space_constraint(value, pltpu.HBM) for value in inputs]
    applied, coarse = pl.pallas_call(
        functools.partial(kernel, nx, ny),
        out_shape=(
            jax.ShapeDtypeStruct(traces.shape, F32),
            jax.ShapeDtypeStruct((RHS * COMPS, 128), F32),
        ),
        in_specs=[pl.BlockSpec(memory_space=pltpu.HBM)] * 8,
        out_specs=(pl.BlockSpec(memory_space=vmem), pl.BlockSpec(memory_space=vmem)),
        scratch_shapes=[
            vmem((SUBS, 6, RHS, width), BF16),
            vmem((width, width), BF16),
            vmem((width, width), BF16),
            vmem((width, width), BF16),
            vmem((6, KEYS, width), BF16),
            pltpu.SMEM((SUBS,), F32),
            pltpu.SMEM((SUBS, 4), jnp.int32),
            pltpu.SMEM((SUBS, CORNERS), jnp.int32),
            vmem((2, 6, SUBS, HALF, width), F32),
            vmem((2, 4, size, width), BF16),
            vmem((2, 4, size, width), BF16),
            vmem((6 * size, width), BF16),
            vmem((6 * size, width), F32),
            vmem((6 * size, width), F32),
            vmem((6 * size, width), F32),
            vmem((2, 6, size, width), BF16),
            vmem((2, 4, size, width), BF16),
            vmem((8 * BLOCK, width), BF16),
            vmem((8 * BLOCK, width), BF16),
            vmem((SUBS, 6, RHS, 8 * BLOCK), F32),
            vmem((4, RHS, 128), F32),
            vmem((4, RHS, 128), F32),
            vmem((nz, 12, 128), F32),
            vmem((nz, 12, 128), F32),
            vmem((12, 128), F32),
            vmem((QUAD, 12, 128), F32),
            dma((8,)),
            dma((2, 4)),
            dma((2, 4)),
            dma((2, 4)),
            dma((2, 4)),
            dma((4,)),
            dma((4,)),
            dma((nz,)),
            dma((nz,)),
            dma((QUAD,)),
            dma((QUAD,)),
            pltpu.SemaphoreType.REGULAR,
        ],
        compiler_params=pltpu.CompilerParams(
            collective_id=0, has_side_effects=True, vmem_limit_bytes=40 * 2**20
        ),
    )(*inputs)
    return applied, coarse[:, :8]


def solution(mesh):
    return jax.shard_map(
        body,
        mesh=mesh,
        in_specs=(
            P("sx", "sy", None, None, None, None),
            P("sx", "sy", None),
            P("sx", "sy", None, None),
            P("sx", "sy", None, None),
            P(),
            P(),
            P(),
            P(),
        ),
        out_specs=(P("sx", "sy", None, None, None, None), P(None, ("sx", "sy"))),
        check_vma=False,
    )
```

```python
import functools

import jax
import jax.numpy as jnp
from jax import lax
from jax.experimental import pallas as pl
from jax.experimental.pallas import tpu as pltpu
from jax.sharding import PartitionSpec as P

MESH = pl.DeviceIdType.MESH
F32, BF16 = jnp.float32, jnp.bfloat16
SUBS = 4
RHS = 16
HALF = 8
CORNERS = 8
COMPS = 3
KEYS = CORNERS * COMPS
BLOCK = 32
QUAD = 4
OPP = (1, 0, 3, 2, 5, 4)


def nt_dot(left, right):
    return lax.dot_general(left, right, (((1,), (1,)), ((), ())), preferred_element_type=F32)


def split(value, parts):
    out = []
    for _ in range(parts):
        head = value.astype(BF16)
        out.append(head)
        value = value - head.astype(F32)
    return out


def kernel(
    nx, ny,
    traces, visc_in, partner_in, owner_in, self_in, opp_in, cross_in, cmap_in,
    applied, coarse,
    raw, s_mat, o_mat, c_mat, cmap, visc, partner, owner,
    own, out1, in1, jump, w_s, w_o, w_c, local, in2,
    w_hi, w_lo, y_all, y_out, y_in, stacked, dense, z_in,
    load_sem, send1, recv1, send2, recv2, send_y, recv_y, send_z, recv_z, far_sem,
):
    width = raw.shape[-1]
    sx, sy = lax.axis_index("sx"), lax.axis_index("sy")
    z = sy // QUAD

    def in_row(to):
        return (sx, lax.rem(to + ny, ny))

    beside = (
        (lax.rem(sx + 1, nx), sy),
        (lax.rem(sx + nx - 1, nx), sy),
        in_row(sy + 1),
        in_row(sy - 1),
    )
    inside = (sx < nx - 1, sx > 0, sy < ny - 1, sy > 0)

    barrier = pltpu.get_barrier_semaphore()

    def signal(semaphore, device):
        pl.semaphore_signal(semaphore, inc=1, device_id=device, device_id_type=MESH)

    with jax.named_scope("greet"):
        for f in range(4):
            pl.when(inside[f])(functools.partial(signal, barrier, beside[f]))

    loads = {}
    for i, (name, source, target) in enumerate((
        ("raw", traces.at[0, 0], raw),
        ("cmap", cmap_in, cmap),
        ("cross", cross_in, c_mat),
        ("self", self_in, s_mat),
        ("opp", opp_in, o_mat),
        ("visc", visc_in.at[0, 0], visc),
        ("partner", partner_in.at[0, 0], partner),
        ("owner", owner_in.at[0, 0], owner),
    )):
        loads[name] = pltpu.make_async_copy(source, target, load_sem.at[i])
        loads[name].start()

    known = (z + 1) * QUAD

    def to_others(first, last, act):
        @pl.loop(first, last)
        def _(to):
            pl.when(to != sy)(lambda: act(to))

    with jax.named_scope("greet_row"):
        to_others(z * QUAD, ny, lambda to: signal(barrier, (sx, to)))

    def exchange(source, target, sends, recvs, f):
        copy = pltpu.make_async_remote_copy(
            src_ref=source,
            dst_ref=target.at[OPP[f]],
            send_sem=sends.at[f],
            recv_sem=recvs.at[OPP[f]],
            device_id=beside[f],
            device_id_type=MESH,
        )
        pl.when(inside[f])(copy.start)
        return (
            lambda: pl.when(inside[OPP[f]])(copy.wait_recv),
            lambda: pl.when(inside[f])(copy.wait_send),
        )

    lane = lax.broadcasted_iota(jnp.int32, (1, 128), 1)
    block = lane // BLOCK

    def moved(value, shift):
        shift = (shift * BLOCK) % 128
        return pltpu.roll(value, shift, 1) if shift else value

    with jax.named_scope("weights"):
        loads["cmap"].wait()
        pad = jnp.zeros((BLOCK - KEYS, width), F32)
        faces = [jnp.concatenate([cmap[f].astype(F32), pad], 0) for f in range(6)]
        straight = jnp.concatenate(faces, 0).astype(BF16)
        products = []
        for name, matrix in (("cross", c_mat), ("self", s_mat), ("opp", o_mat)):
            loads[name].wait()
            product = nt_dot(straight, matrix[...])
            products.append([product[f * BLOCK : (f + 1) * BLOCK] for f in range(6)])
        cross, same, across = products
        pairs = [cross[0] + cross[1], cross[2] + cross[3], cross[4] + cross[5]]
        adjacent = [pairs[1] + pairs[2], pairs[0] + pairs[2], pairs[0] + pairs[1]]
        weight = [same[f] + across[OPP[f]] + adjacent[f // 2] for f in range(6)]
        weight.append(jnp.zeros((2 * BLOCK, width), F32))
        w_hi[...], w_lo[...] = split(jnp.concatenate(weight, 0), 2)

    def value_of(s, f, face, to):
        tile = y_all[s, f, :, face // 4 * 128 : face // 4 * 128 + 128]
        return jnp.where(block == to, moved(tile, to - face % 4), 0.0)

    with jax.named_scope("values"):
        loads["raw"].wait()
        flat = raw[...].reshape(SUBS * 6 * RHS, width)
        both = nt_dot(flat, w_hi[...]) + nt_dot(flat, w_lo[...])
        y_all[...] = both.reshape(SUBS, 6, RHS, 8 * BLOCK)
        for f in range(4):
            y_out[f] = sum(value_of(s, f, OPP[f], s) for s in range(SUBS))

    with jax.named_scope("entry"):
        pl.semaphore_wait(barrier, sum(here.astype(jnp.int32) for here in inside) + known - 1)

    copies_y = [exchange(y_out.at[f], y_in, send_y, recv_y, f) for f in range(4)]
    with jax.named_scope("repack"):
        for f in range(6):
            for s in range(SUBS):
                both = raw[s, f].astype(F32)
                for c in range(2):
                    own[c, f, s] = both[c * HALF : (c + 1) * HALF]
            if f < 4:
                for c in range(2):
                    out1[c, f] = own[c, f].reshape(SUBS * HALF, width).astype(BF16)

    copies1 = [
        [exchange(out1.at[c, f], in1.at[c], send1.at[c], recv1.at[c], f) for f in range(4)]
        for c in range(2)
    ]

    to_others(0, z * QUAD, lambda to: signal(far_sem, (sx, to)))

    for f in range(4):
        def clear(f=f):
            y_in[f] = jnp.zeros(y_in.shape[1:], F32)
            for ref in (in1, in2):
                for c in range(2):
                    ref[c, f] = jnp.zeros(ref.shape[2:], BF16)

        pl.when(jnp.logical_not(inside[f]))(clear)

    with jax.named_scope("owners"):
        for name in ("visc", "partner", "owner"):
            loads[name].wait()
        visc_lanes = jnp.zeros((1, 128), F32)
        for s in range(SUBS):
            visc_lanes = jnp.where(block == s, visc[s], visc_lanes)
        owners = jnp.full((1, 128), -1, jnp.int32)
        for s in range(SUBS):
            for m in range(CORNERS):
                first = s * BLOCK + m * COMPS
                owners = jnp.where((lane >= first) & (lane < first + COMPS), owner[s, m], owners)
        unknown = lax.broadcasted_iota(jnp.int32, (8 * ny, 1), 0)
        onehot = jnp.where(unknown == owners, 1.0, 0.0).astype(BF16)
        parts = jnp.zeros((RHS, 128), F32)
        for s in range(SUBS):
            for f in range(6):
                parts += value_of(s, f, f, s)
            if s < SUBS - 1:
                parts -= value_of(s + 1, 5, 4, s)
            if s > 0:
                parts -= value_of(s - 1, 4, 5, s)

    with jax.named_scope("wait_values"):
        for wait, _ in copies_y:
            wait()

    with jax.named_scope("corners"):
        for f in range(4):
            received = y_in[f]
            slots = jnp.zeros((1, 128), jnp.int32)
            for s in range(SUBS):
                slots = jnp.where(block == s, partner[s, f], slots)
            for d in range(SUBS):
                here = slots == lax.rem(block - d + SUBS, SUBS)
                parts -= jnp.where(here, moved(received, d), 0.0)
        parts = parts * visc_lanes
        comp = lax.rem(lax.rem(lane, BLOCK), COMPS)
        for c in range(COMPS):
            stacked[pl.ds(c, RHS, stride=COMPS)] = jnp.where(comp == c, parts, 0.0)
        pieces = split(stacked[...], 3)
        total = sum(nt_dot(onehot, piece) for piece in pieces)
        total = total.reshape(ny, 8, RHS * COMPS)
        total = jnp.concatenate([total, jnp.zeros((ny, 8, 128 - RHS * COMPS), F32)], 2)
        for to in range(ny):
            tile = total[to]
            dense[to] = jnp.where(lane < 64, tile[:4], pltpu.roll(tile[4:], 64, 1))

    def corner_copy(to):
        return pltpu.make_async_remote_copy(
            src_ref=dense.at[to],
            dst_ref=z_in.at[sy],
            send_sem=send_z.at[to],
            recv_sem=recv_z.at[sy],
            device_id=(sx, to),
            device_id_type=MESH,
        )

    def corner_arrival(source):
        return pltpu.make_async_remote_copy(
            src_ref=dense.at[source],
            dst_ref=z_in.at[source],
            send_sem=send_z.at[source],
            recv_sem=recv_z.at[source],
            device_id=(sx, source),
            device_id_type=MESH,
        )

    with jax.named_scope("corner_send"):
        to_others(0, known, lambda to: corner_copy(to).start())

    def selected(f, received):
        received = received.astype(F32)
        slots = [received[p * HALF : (p + 1) * HALF] for p in range(SUBS)]
        values = []
        for s in range(SUBS):
            value = slots[0]
            for p in range(1, SUBS):
                value = jnp.where(partner[s, f] == p, slots[p], value)
            values.append(value)
        return jnp.concatenate(values, 0)

    none = jnp.zeros((HALF, width), F32)
    visc_rows = jnp.concatenate([jnp.full((HALF, width), visc[s], F32) for s in range(SUBS)], 0)
    size = SUBS * HALF

    copies2 = []
    for c in range(2):
        with jax.named_scope(f"wait_traces{c}"):
            for wait, _ in copies1[c]:
                wait()
        with jax.named_scope(f"local{c}"):
            for f in range(4):
                mine = own[c, f].reshape(size, width)
                jump[f * size : (f + 1) * size] = (mine - selected(f, in1[c, f])).astype(BF16)
            top, bottom = own[c, 4].reshape(size, width), own[c, 5].reshape(size, width)
            above = jnp.concatenate([bottom[HALF:], none], 0)
            below = jnp.concatenate([none, top[:-HALF]], 0)
            jump[4 * size : 5 * size] = (top - above).astype(BF16)
            jump[5 * size : 6 * size] = (bottom - below).astype(BF16)
            w_c[...] = jnp.dot(jump[...], c_mat[...], preferred_element_type=F32)
            w_s[...] = jnp.dot(jump[...], s_mat[...], preferred_element_type=F32)
            w_o[...] = jnp.dot(jump[...], o_mat[...], preferred_element_type=F32)

            def face(ref, f):
                return ref[f * size : (f + 1) * size]

            copies2.append([])
            for f in range(6):
                others = [g for g in range(6) if g // 2 != f // 2]
                value = face(w_s, f) + face(w_o, OPP[f])
                value += (face(w_c, others[0]) + face(w_c, others[1])) + (
                    face(w_c, others[2]) + face(w_c, others[3])
                )
                local[c, f] = (visc_rows * value).astype(BF16)
                if f < 4:
                    copies2[c].append(exchange(local.at[c, f], in2.at[c], send2.at[c], recv2.at[c], f))
            top, bottom = local[c, 4].astype(F32), local[c, 5].astype(F32)
            above = jnp.concatenate([bottom[HALF:], none], 0)
            below = jnp.concatenate([none, top[:-HALF]], 0)
            for f, value in ((4, top - above), (5, bottom - below)):
                for s in range(SUBS):
                    applied[0, 0, s, f, c * HALF : (c + 1) * HALF] = value[s * HALF : (s + 1) * HALF]

    def finish(c):
        with jax.named_scope(f"wait_local{c}"):
            for wait, _ in copies2[c]:
                wait()
        with jax.named_scope(f"applied{c}"):
            for f in range(4):
                value = local[c, f].astype(F32) - selected(f, in2[c, f])
                for s in range(SUBS):
                    applied[0, 0, s, f, c * HALF : (c + 1) * HALF] = value[s * HALF : (s + 1) * HALF]

    with jax.named_scope("far"):
        pl.when(known < ny)(lambda: pl.semaphore_wait(far_sem, ny - known))
        to_others(known, ny, lambda to: corner_copy(to).start())

    finish(0)
    finish(1)

    with jax.named_scope("corner_wait"):
        to_others(0, ny, lambda source: corner_arrival(source).wait_recv())
    with jax.named_scope("corner_sum"):
        result = jnp.zeros((4, 128), F32)
        for source in range(ny):
            result += jnp.where(sy == source, dense[source], z_in[source])
        coarse[:4] = result
        coarse[4:] = pltpu.roll(result, 64, 1)

    with jax.named_scope("sent"):
        to_others(0, ny, lambda to: corner_copy(to).wait_send())
        for _, wait in [*copies_y, *copies1[0], *copies1[1], *copies2[0], *copies2[1]]:
            wait()


def body(traces, viscosity, partner, corner_owner, self_block, opposite_block, cross_block, corner_map):
    nx, ny = lax.axis_size("sx"), lax.axis_size("sy")
    width = traces.shape[-1]
    vmem, dma = pltpu.VMEM, pltpu.SemaphoreType.DMA
    size = SUBS * HALF
    inputs = (
        traces, viscosity, partner, corner_owner, self_block, opposite_block, cross_block,
        jnp.transpose(corner_map, (1, 0, 2)),
    )
    inputs = [pltpu.with_memory_space_constraint(value, pltpu.HBM) for value in inputs]
    applied, coarse = pl.pallas_call(
        functools.partial(kernel, nx, ny),
        out_shape=(
            jax.ShapeDtypeStruct(traces.shape, F32),
            jax.ShapeDtypeStruct((8, 128), F32),
        ),
        in_specs=[pl.BlockSpec(memory_space=pltpu.HBM)] * 8,
        out_specs=(pl.BlockSpec(memory_space=vmem), pl.BlockSpec(memory_space=vmem)),
        scratch_shapes=[
            vmem((SUBS, 6, RHS, width), BF16),
            vmem((width, width), BF16),
            vmem((width, width), BF16),
            vmem((width, width), BF16),
            vmem((6, KEYS, width), BF16),
            pltpu.SMEM((SUBS,), F32),
            pltpu.SMEM((SUBS, 4), jnp.int32),
            pltpu.SMEM((SUBS, CORNERS), jnp.int32),
            vmem((2, 6, SUBS, HALF, width), F32),
            vmem((2, 4, size, width), BF16),
            vmem((2, 4, size, width), BF16),
            vmem((6 * size, width), BF16),
            vmem((6 * size, width), F32),
            vmem((6 * size, width), F32),
            vmem((6 * size, width), F32),
            vmem((2, 6, size, width), BF16),
            vmem((2, 4, size, width), BF16),
            vmem((8 * BLOCK, width), BF16),
            vmem((8 * BLOCK, width), BF16),
            vmem((SUBS, 6, RHS, 8 * BLOCK), F32),
            vmem((4, RHS, 128), F32),
            vmem((4, RHS, 128), F32),
            vmem((RHS * COMPS, 128), F32),
            vmem((ny, 4, 128), F32),
            vmem((ny, 4, 128), F32),
            dma((8,)),
            dma((2, 4)),
            dma((2, 4)),
            dma((2, 4)),
            dma((2, 4)),
            dma((4,)),
            dma((4,)),
            dma((ny,)),
            dma((ny,)),
            pltpu.SemaphoreType.REGULAR,
        ],
        compiler_params=pltpu.CompilerParams(
            collective_id=0, has_side_effects=True, vmem_limit_bytes=40 * 2**20
        ),
    )(*inputs)
    return applied, coarse[:, : RHS * COMPS].T


def solution(mesh):
    return jax.shard_map(
        body,
        mesh=mesh,
        in_specs=(
            P("sx", "sy", None, None, None, None),
            P("sx", "sy", None),
            P("sx", "sy", None, None),
            P("sx", "sy", None, None),
            P(),
            P(),
            P(),
            P(),
        ),
        out_specs=(P("sx", "sy", None, None, None, None), P(None, ("sx", "sy"))),
        check_vma=False,
    )
```

```python
import functools

import jax
import jax.numpy as jnp
from jax import lax
from jax.experimental import pallas as pl
from jax.experimental.pallas import tpu as pltpu
from jax.sharding import PartitionSpec as P

MESH = pl.DeviceIdType.MESH
F32, BF16 = jnp.float32, jnp.bfloat16
SUBS = 4
RHS = 16
HALF = 8
CORNERS = 8
COMPS = 3
KEYS = CORNERS * COMPS
BLOCK = 32
QUAD = 4
OPP = (1, 0, 3, 2, 5, 4)
FIRST = 4 * QUAD


def nt_dot(left, right):
    return lax.dot_general(left, right, (((1,), (1,)), ((), ())), preferred_element_type=F32)


def split(value, parts):
    out = []
    for _ in range(parts):
        head = value.astype(BF16)
        out.append(head)
        value = value - head.astype(F32)
    return out


def kernel(
    nx, ny,
    traces, visc_in, partner_in, owner_in, self_in, opp_in, cross_in, cmap_in,
    applied, coarse,
    raw, s_mat, o_mat, c_mat, cmap, visc, partner, owner,
    own, out1, in1, jump, w_s, w_o, w_c, local, in2,
    w_hi, w_lo, y_all, y_out, y_in, stacked, dense, z_in,
    load_sem, send, recv, share_sem, far_sem,
):
    width = raw.shape[-1]
    sx, sy = lax.axis_index("sx"), lax.axis_index("sy")
    z = sy // QUAD

    def in_row(to):
        return (sx, lax.rem(to + ny, ny))

    beside = (
        (lax.rem(sx + 1, nx), sy),
        (lax.rem(sx + nx - 1, nx), sy),
        in_row(sy + 1),
        in_row(sy - 1),
    )
    inside = (sx < nx - 1, sx > 0, sy < ny - 1, sy > 0)

    barrier = pltpu.get_barrier_semaphore()

    def signal(semaphore, device):
        pl.semaphore_signal(semaphore, inc=1, device_id=device, device_id_type=MESH)

    with jax.named_scope("greet"):
        for f in range(4):
            pl.when(inside[f])(functools.partial(signal, barrier, beside[f]))

    loads = {}
    for i, (name, source, target) in enumerate((
        ("cmap", cmap_in, cmap),
        ("cross", cross_in, c_mat),
        ("self", self_in, s_mat),
        ("opp", opp_in, o_mat),
        ("raw", traces.at[0, 0], raw),
        ("visc", visc_in.at[0, 0], visc),
        ("partner", partner_in.at[0, 0], partner),
        ("owner", owner_in.at[0, 0], owner),
    )):
        loads[name] = pltpu.make_async_copy(source, target, load_sem.at[i])
        loads[name].start()

    known = (z + 1) * QUAD

    def to_others(first, last, act):
        @pl.loop(first, last)
        def _(to):
            pl.when(to != sy)(lambda: act(to))

    with jax.named_scope("greet_row"):
        to_others(z * QUAD, ny, lambda to: signal(barrier, (sx, to)))

    count = sum(here.astype(jnp.int32) for here in inside)

    def exchange(step, source, target, f):
        copy = pltpu.make_async_remote_copy(
            src_ref=source.at[f],
            dst_ref=target.at[OPP[f]],
            send_sem=send.at[step],
            recv_sem=recv.at[step],
            device_id=beside[f],
            device_id_type=MESH,
        )
        pl.when(inside[f])(copy.start)

    def arrival(step, source, target):
        copies = [
            pltpu.make_async_remote_copy(
                src_ref=source.at[pl.ds(0, k)],
                dst_ref=target.at[pl.ds(0, k)],
                send_sem=send.at[step],
                recv_sem=recv.at[step],
                device_id=beside[0],
                device_id_type=MESH,
            )
            for k in (2, 3, 4)
        ]

        def wait(which):
            for k, copy in zip((2, 3, 4), copies):
                pl.when(count == k)(getattr(copy, which))

        return wait

    steps = [
        (0, y_out, y_in),
        (1, out1.at[0], in1.at[0]),
        (2, out1.at[1], in1.at[1]),
        (3, local.at[0], in2.at[0]),
        (4, local.at[1], in2.at[1]),
    ]
    arrivals = [arrival(*step) for step in steps]

    lane = lax.broadcasted_iota(jnp.int32, (1, 128), 1)
    block = lane // BLOCK

    def moved(value, shift):
        shift = (shift * BLOCK) % 128
        return pltpu.roll(value, shift, 1) if shift else value

    with jax.named_scope("corner_map"):
        loads["cmap"].wait()
        pad = jnp.zeros((BLOCK - KEYS, width), F32)
        faces = [jnp.concatenate([cmap[f].astype(F32), pad], 0) for f in range(6)]
        straight = jnp.concatenate(faces, 0).astype(BF16)

    def through(name, matrix):
        loads[name].wait()
        product = nt_dot(straight, matrix[...])
        return [product[f * BLOCK : (f + 1) * BLOCK] for f in range(6)]

    with jax.named_scope("weights_cross"):
        cross = through("cross", c_mat)
    with jax.named_scope("weights_self"):
        same = through("self", s_mat)
    with jax.named_scope("weights_opposite"):
        across = through("opp", o_mat)
        pairs = [cross[0] + cross[1], cross[2] + cross[3], cross[4] + cross[5]]
        adjacent = [pairs[1] + pairs[2], pairs[0] + pairs[2], pairs[0] + pairs[1]]
        weight = [same[f] + across[OPP[f]] + adjacent[f // 2] for f in range(6)]
        weight.append(jnp.zeros((2 * BLOCK, width), F32))
        w_hi[...], w_lo[...] = split(jnp.concatenate(weight, 0), 2)

    def value_of(s, f, face, to):
        tile = y_all[s, f, :, face // 4 * 128 : face // 4 * 128 + 128]
        return jnp.where(block == to, moved(tile, to - face % 4), 0.0)

    def values(f):
        flat = raw[:, f : f + 2].reshape(SUBS * 2 * RHS, width)
        both = nt_dot(flat, w_hi[...]) + nt_dot(flat, w_lo[...])
        y_all[:, f : f + 2] = both.reshape(SUBS, 2, RHS, 8 * BLOCK)

    for f in (0, 2):
        with jax.named_scope(f"values{f}"):
            if f == 0:
                loads["raw"].wait()
            values(f)
            for to in (f, f + 1):
                y_out[to] = sum(value_of(s, to, OPP[to], s) for s in range(SUBS))
        if f == 0:
            with jax.named_scope("entry"):
                pl.semaphore_wait(barrier, count + known - 1)
        for to in (f, f + 1):
            exchange(*steps[0], to)

    with jax.named_scope("repack"):
        for f in range(6):
            for s in range(SUBS):
                both = raw[s, f].astype(F32)
                for c in range(2):
                    own[c, f, s] = both[c * HALF : (c + 1) * HALF]
            if f < 4:
                for c in range(2):
                    out1[c, f] = own[c, f].reshape(SUBS * HALF, width).astype(BF16)

    for c in range(2):
        for f in range(4):
            exchange(*steps[1 + c], f)
    to_others(0, z * QUAD, lambda to: signal(far_sem, (sx, to)))

    for f in range(4):
        def clear(f=f):
            y_in[f] = jnp.zeros(y_in.shape[1:], F32)
            for ref in (in1, in2):
                for c in range(2):
                    ref[c, f] = jnp.zeros(ref.shape[2:], BF16)

        pl.when(jnp.logical_not(inside[f]))(clear)

    with jax.named_scope("owners"):
        for name in ("visc", "partner", "owner"):
            loads[name].wait()
        visc_lanes = jnp.zeros((1, 128), F32)
        for s in range(SUBS):
            visc_lanes = jnp.where(block == s, visc[s], visc_lanes)
        owners = jnp.full((1, 128), -1, jnp.int32)
        for s in range(SUBS):
            for m in range(CORNERS):
                first = s * BLOCK + m * COMPS
                owners = jnp.where((lane >= first) & (lane < first + COMPS), owner[s, m], owners)
        unknown = lax.broadcasted_iota(jnp.int32, (8 * ny, 1), 0)
        onehot = jnp.where(unknown == owners, 1.0, 0.0).astype(BF16)
        values(4)
        parts = jnp.zeros((RHS, 128), F32)
        for s in range(SUBS):
            for f in range(6):
                parts += value_of(s, f, f, s)
            if s < SUBS - 1:
                parts -= value_of(s + 1, 5, 4, s)
            if s > 0:
                parts -= value_of(s - 1, 4, 5, s)

    with jax.named_scope("wait_values"):
        arrivals[0]("wait_recv")

    with jax.named_scope("corners"):
        for f in range(4):
            received = y_in[f]
            slots = jnp.zeros((1, 128), jnp.int32)
            for s in range(SUBS):
                slots = jnp.where(block == s, partner[s, f], slots)
            for d in range(SUBS):
                here = slots == lax.rem(block - d + SUBS, SUBS)
                parts -= jnp.where(here, moved(received, d), 0.0)
        parts = parts * visc_lanes
        comp = lax.rem(lax.rem(lane, BLOCK), COMPS)
        for c in range(COMPS):
            stacked[pl.ds(c, RHS, stride=COMPS)] = jnp.where(comp == c, parts, 0.0)
        pieces = split(stacked[...], 3)

    def assemble(first, last):
        total = sum(nt_dot(onehot[first * 8 : last * 8], piece) for piece in pieces)
        total = total.reshape(last - first, 8, RHS * COMPS)
        pad = jnp.zeros((last - first, 8, 128 - RHS * COMPS), F32)
        total = jnp.concatenate([total, pad], 2)
        for to in range(first, last):
            tile = total[to - first]
            dense[to] = jnp.where(lane < 64, tile[:4], pltpu.roll(tile[4:], 64, 1))

    def corner_copy(to):
        return pltpu.make_async_remote_copy(
            src_ref=dense.at[to],
            dst_ref=z_in.at[sy],
            send_sem=share_sem.at[0],
            recv_sem=share_sem.at[1],
            device_id=(sx, to),
            device_id_type=MESH,
        )

    shares = pltpu.make_async_remote_copy(
        src_ref=dense.at[pl.ds(0, ny - 1)],
        dst_ref=z_in.at[pl.ds(0, ny - 1)],
        send_sem=share_sem.at[0],
        recv_sem=share_sem.at[1],
        device_id=beside[0],
        device_id_type=MESH,
    )

    with jax.named_scope("corner_send"):
        assemble(0, FIRST)
        to_others(0, jnp.minimum(known, FIRST), lambda to: corner_copy(to).start())
    if FIRST < ny:
        with jax.named_scope("corner_rest"):
            assemble(FIRST, ny)

    def selected(f, received):
        received = received.astype(F32)
        slots = [received[p * HALF : (p + 1) * HALF] for p in range(SUBS)]
        values = []
        for s in range(SUBS):
            value = slots[0]
            for p in range(1, SUBS):
                value = jnp.where(partner[s, f] == p, slots[p], value)
            values.append(value)
        return jnp.concatenate(values, 0)

    none = jnp.zeros((HALF, width), F32)
    visc_rows = jnp.concatenate([jnp.full((HALF, width), visc[s], F32) for s in range(SUBS)], 0)
    size = SUBS * HALF

    for c in range(2):
        with jax.named_scope(f"wait_traces{c}"):
            arrivals[1 + c]("wait_recv")
        with jax.named_scope(f"local{c}"):
            for f in range(4):
                mine = own[c, f].reshape(size, width)
                jump[f * size : (f + 1) * size] = (mine - selected(f, in1[c, f])).astype(BF16)
            top, bottom = own[c, 4].reshape(size, width), own[c, 5].reshape(size, width)
            above = jnp.concatenate([bottom[HALF:], none], 0)
            below = jnp.concatenate([none, top[:-HALF]], 0)
            jump[4 * size : 5 * size] = (top - above).astype(BF16)
            jump[5 * size : 6 * size] = (bottom - below).astype(BF16)
            w_c[...] = jnp.dot(jump[...], c_mat[...], preferred_element_type=F32)
            w_s[...] = jnp.dot(jump[...], s_mat[...], preferred_element_type=F32)
            w_o[...] = jnp.dot(jump[...], o_mat[...], preferred_element_type=F32)

            def face(ref, f):
                return ref[f * size : (f + 1) * size]

            for f in range(6):
                others = [g for g in range(6) if g // 2 != f // 2]
                value = face(w_s, f) + face(w_o, OPP[f])
                value += (face(w_c, others[0]) + face(w_c, others[1])) + (
                    face(w_c, others[2]) + face(w_c, others[3])
                )
                local[c, f] = (visc_rows * value).astype(BF16)
                if f < 4:
                    exchange(*steps[3 + c], f)
            top, bottom = local[c, 4].astype(F32), local[c, 5].astype(F32)
            above = jnp.concatenate([bottom[HALF:], none], 0)
            below = jnp.concatenate([none, top[:-HALF]], 0)
            for f, value in ((4, top - above), (5, bottom - below)):
                for s in range(SUBS):
                    applied[0, 0, s, f, c * HALF : (c + 1) * HALF] = value[s * HALF : (s + 1) * HALF]
        if c == 0:
            with jax.named_scope("corner_send_rest"):
                to_others(FIRST, known, lambda to: corner_copy(to).start())

    def finish(c):
        with jax.named_scope(f"wait_local{c}"):
            arrivals[3 + c]("wait_recv")
        with jax.named_scope(f"applied{c}"):
            for f in range(4):
                value = local[c, f].astype(F32) - selected(f, in2[c, f])
                for s in range(SUBS):
                    applied[0, 0, s, f, c * HALF : (c + 1) * HALF] = value[s * HALF : (s + 1) * HALF]

    with jax.named_scope("far"):
        pl.when(known < ny)(lambda: pl.semaphore_wait(far_sem, ny - known))
        to_others(known, ny, lambda to: corner_copy(to).start())

    finish(0)
    finish(1)

    with jax.named_scope("corner_wait"):
        shares.wait_recv()
    with jax.named_scope("corner_sum"):
        result = jnp.zeros((4, 128), F32)
        for source in range(ny):
            result += jnp.where(sy == source, dense[source], z_in[source])
        coarse[:4] = result[:, : RHS * COMPS]
        coarse[4:] = pltpu.roll(result, 64, 1)[:, : RHS * COMPS]

    with jax.named_scope("sent"):
        shares.wait_send()
        for wait in arrivals:
            wait("wait_send")


def write_out(applied, coarse, applied_out, coarse_out, sems):
    copies = (
        pltpu.make_async_copy(applied, applied_out, sems.at[0]),
        pltpu.make_async_copy(coarse, coarse_out, sems.at[1]),
    )
    for copy in copies:
        copy.start()
    for copy in copies:
        copy.wait()


def body(traces, viscosity, partner, corner_owner, self_block, opposite_block, cross_block, corner_map):
    nx, ny = lax.axis_size("sx"), lax.axis_size("sy")
    width = traces.shape[-1]
    vmem, dma = pltpu.VMEM, pltpu.SemaphoreType.DMA
    size = SUBS * HALF
    inputs = (
        traces, viscosity, partner, corner_owner, self_block, opposite_block, cross_block,
        jnp.transpose(corner_map, (1, 0, 2)),
    )
    inputs = [pltpu.with_memory_space_constraint(value, pltpu.HBM) for value in inputs]
    applied, coarse = pl.pallas_call(
        functools.partial(kernel, nx, ny),
        out_shape=(
            jax.ShapeDtypeStruct(traces.shape, F32),
            jax.ShapeDtypeStruct((8, RHS * COMPS), F32),
        ),
        in_specs=[pl.BlockSpec(memory_space=pltpu.HBM)] * 8,
        out_specs=(pl.BlockSpec(memory_space=vmem), pl.BlockSpec(memory_space=vmem)),
        scratch_shapes=[
            vmem((SUBS, 6, RHS, width), BF16),
            vmem((width, width), BF16),
            vmem((width, width), BF16),
            vmem((width, width), BF16),
            vmem((6, KEYS, width), BF16),
            pltpu.SMEM((SUBS,), F32),
            pltpu.SMEM((SUBS, 4), jnp.int32),
            pltpu.SMEM((SUBS, CORNERS), jnp.int32),
            vmem((2, 6, SUBS, HALF, width), F32),
            vmem((2, 4, size, width), BF16),
            vmem((2, 4, size, width), BF16),
            vmem((6 * size, width), BF16),
            vmem((6 * size, width), F32),
            vmem((6 * size, width), F32),
            vmem((6 * size, width), F32),
            vmem((2, 6, size, width), BF16),
            vmem((2, 4, size, width), BF16),
            vmem((8 * BLOCK, width), BF16),
            vmem((8 * BLOCK, width), BF16),
            vmem((SUBS, 6, RHS, 8 * BLOCK), F32),
            vmem((4, RHS, 128), F32),
            vmem((4, RHS, 128), F32),
            vmem((RHS * COMPS, 128), F32),
            vmem((ny, 4, 128), F32),
            vmem((ny, 4, 128), F32),
            dma((8,)),
            dma((5,)),
            dma((5,)),
            dma((2,)),
            pltpu.SemaphoreType.REGULAR,
        ],
        compiler_params=pltpu.CompilerParams(
            collective_id=0, has_side_effects=True, vmem_limit_bytes=40 * 2**20
        ),
    )(*inputs)
    applied, coarse = pl.pallas_call(
        write_out,
        out_shape=tuple(jax.ShapeDtypeStruct(value.shape, F32) for value in (applied, coarse)),
        in_specs=[pl.BlockSpec(memory_space=pltpu.VMEM)] * 2,
        out_specs=(pl.BlockSpec(memory_space=pltpu.HBM),) * 2,
        scratch_shapes=[dma((2,))],
    )(*(pltpu.with_memory_space_constraint(value, pltpu.VMEM) for value in (applied, coarse)))
    return applied, coarse.T


def solution(mesh):
    return jax.shard_map(
        body,
        mesh=mesh,
        in_specs=(
            P("sx", "sy", None, None, None, None),
            P("sx", "sy", None),
            P("sx", "sy", None, None),
            P("sx", "sy", None, None),
            P(),
            P(),
            P(),
            P(),
        ),
        out_specs=(P("sx", "sy", None, None, None, None), P(None, ("sx", "sy"))),
        check_vma=False,
    )
```

```python
import functools

import jax
import jax.numpy as jnp
from jax import lax
from jax.experimental import pallas as pl
from jax.experimental.pallas import tpu as pltpu
from jax.sharding import PartitionSpec as P

MESH = pl.DeviceIdType.MESH
F32, BF16 = jnp.float32, jnp.bfloat16
SUBS = 4
RHS = 16
HALF = 8
CORNERS = 8
COMPS = 3
KEYS = CORNERS * COMPS
BLOCK = 32
QUAD = 4
OPP = (1, 0, 3, 2, 5, 4)
FIRST = 4 * QUAD


def nt_dot(left, right):
    return lax.dot_general(left, right, (((1,), (1,)), ((), ())), preferred_element_type=F32)


def split(value, parts):
    out = []
    for _ in range(parts):
        head = value.astype(BF16)
        out.append(head)
        value = value - head.astype(F32)
    return out


def kernel(
    nx, ny,
    traces, visc_in, partner_in, owner_in, self_in, opp_in, cross_in, cmap_in,
    applied, coarse,
    raw, s_mat, o_mat, c_mat, cmap, visc, partner, owner,
    own, out1, in1, jump, w_s, w_o, w_c, local, in2,
    w_hi, w_lo, y_all, y_out, y_in, stacked, dense, z_in,
    load_sem, send, recv, share_sem, far_sem,
):
    width = raw.shape[-1]
    sx, sy = lax.axis_index("sx"), lax.axis_index("sy")
    z = sy // QUAD

    def in_row(to):
        return (sx, lax.rem(to + ny, ny))

    beside = (
        (lax.rem(sx + 1, nx), sy),
        (lax.rem(sx + nx - 1, nx), sy),
        in_row(sy + 1),
        in_row(sy - 1),
    )
    inside = (sx < nx - 1, sx > 0, sy < ny - 1, sy > 0)

    barrier = pltpu.get_barrier_semaphore()

    def signal(semaphore, device):
        pl.semaphore_signal(semaphore, inc=1, device_id=device, device_id_type=MESH)

    with jax.named_scope("greet"):
        for f in range(4):
            pl.when(inside[f])(functools.partial(signal, barrier, beside[f]))

    loads = {}
    for i, (name, source, target) in enumerate((
        ("cmap", cmap_in, cmap),
        ("cross", cross_in, c_mat),
        ("self", self_in, s_mat),
        ("opp", opp_in, o_mat),
        ("raw", traces.at[0, 0], raw),
        ("visc", visc_in.at[0, 0], visc),
        ("partner", partner_in.at[0, 0], partner),
        ("owner", owner_in.at[0, 0], owner),
    )):
        loads[name] = pltpu.make_async_copy(source, target, load_sem.at[i])
        loads[name].start()

    known = (z + 1) * QUAD

    def to_others(first, last, act):
        @pl.loop(first, last)
        def _(to):
            pl.when(to != sy)(lambda: act(to))

    with jax.named_scope("greet_row"):
        to_others(z * QUAD, ny, lambda to: signal(barrier, (sx, to)))

    count = sum(here.astype(jnp.int32) for here in inside)

    def exchange(step, source, target, f):
        copy = pltpu.make_async_remote_copy(
            src_ref=source.at[f],
            dst_ref=target.at[OPP[f]],
            send_sem=send.at[step],
            recv_sem=recv.at[step],
            device_id=beside[f],
            device_id_type=MESH,
        )
        pl.when(inside[f])(copy.start)

    def arrival(step, source, target):
        copies = [
            pltpu.make_async_remote_copy(
                src_ref=source.at[pl.ds(0, k)],
                dst_ref=target.at[pl.ds(0, k)],
                send_sem=send.at[step],
                recv_sem=recv.at[step],
                device_id=beside[0],
                device_id_type=MESH,
            )
            for k in (2, 3, 4)
        ]

        def wait(which):
            for k, copy in zip((2, 3, 4), copies):
                pl.when(count == k)(getattr(copy, which))

        return wait

    steps = [
        (0, y_out, y_in),
        (1, out1.at[0], in1.at[0]),
        (2, out1.at[1], in1.at[1]),
        (3, local.at[0], in2.at[0]),
        (4, local.at[1], in2.at[1]),
    ]
    arrivals = [arrival(*step) for step in steps]

    lane = lax.broadcasted_iota(jnp.int32, (1, 128), 1)
    block = lane // BLOCK

    def moved(value, shift):
        shift = (shift * BLOCK) % 128
        return pltpu.roll(value, shift, 1) if shift else value

    with jax.named_scope("corner_map"):
        loads["cmap"].wait()
        pad = jnp.zeros((BLOCK - KEYS, width), F32)
        faces = [jnp.concatenate([cmap[f].astype(F32), pad], 0) for f in range(6)]
        straight = jnp.concatenate(faces, 0).astype(BF16)

    def through(name, matrix):
        loads[name].wait()
        product = nt_dot(straight, matrix[...])
        return [product[f * BLOCK : (f + 1) * BLOCK] for f in range(6)]

    with jax.named_scope("weights_cross"):
        cross = through("cross", c_mat)
    with jax.named_scope("weights_self"):
        same = through("self", s_mat)
    with jax.named_scope("weights_opposite"):
        across = through("opp", o_mat)
        pairs = [cross[0] + cross[1], cross[2] + cross[3], cross[4] + cross[5]]
        adjacent = [pairs[1] + pairs[2], pairs[0] + pairs[2], pairs[0] + pairs[1]]
        weight = [same[f] + across[OPP[f]] + adjacent[f // 2] for f in range(6)]
        weight.append(jnp.zeros((2 * BLOCK, width), F32))
        w_hi[...], w_lo[...] = split(jnp.concatenate(weight, 0), 2)

    def value_of(s, f, face, to):
        tile = y_all[s, f, :, face // 4 * 128 : face // 4 * 128 + 128]
        return jnp.where(block == to, moved(tile, to - face % 4), 0.0)

    def values(f):
        flat = raw[:, f : f + 2].reshape(SUBS * 2 * RHS, width)
        both = nt_dot(flat, w_hi[...]) + nt_dot(flat, w_lo[...])
        y_all[:, f : f + 2] = both.reshape(SUBS, 2, RHS, 8 * BLOCK)

    for f in (0, 2):
        with jax.named_scope(f"values{f}"):
            if f == 0:
                loads["raw"].wait()
            values(f)
            for to in (f, f + 1):
                y_out[to] = sum(value_of(s, to, OPP[to], s) for s in range(SUBS))
        if f == 0:
            with jax.named_scope("entry"):
                pl.semaphore_wait(barrier, count + known - 1)
        for to in (f, f + 1):
            exchange(*steps[0], to)

    with jax.named_scope("repack"):
        for f in range(6):
            for s in range(SUBS):
                both = raw[s, f].astype(F32)
                for c in range(2):
                    own[c, f, s] = both[c * HALF : (c + 1) * HALF]
            if f < 4:
                for c in range(2):
                    out1[c, f] = own[c, f].reshape(SUBS * HALF, width).astype(BF16)

    def send_traces():
        for c in range(2):
            for f in range(4):
                exchange(*steps[1 + c], f)

    pl.when(z < ny // QUAD // 2)(send_traces)
    to_others(0, z * QUAD, lambda to: signal(far_sem, (sx, to)))

    for f in range(4):
        def clear(f=f):
            y_in[f] = jnp.zeros(y_in.shape[1:], F32)
            for ref in (in1, in2):
                for c in range(2):
                    ref[c, f] = jnp.zeros(ref.shape[2:], BF16)

        pl.when(jnp.logical_not(inside[f]))(clear)

    with jax.named_scope("owners"):
        for name in ("visc", "partner", "owner"):
            loads[name].wait()
        visc_lanes = jnp.zeros((1, 128), F32)
        for s in range(SUBS):
            visc_lanes = jnp.where(block == s, visc[s], visc_lanes)
        owners = jnp.full((1, 128), -1, jnp.int32)
        for s in range(SUBS):
            for m in range(CORNERS):
                first = s * BLOCK + m * COMPS
                owners = jnp.where((lane >= first) & (lane < first + COMPS), owner[s, m], owners)
        unknown = lax.broadcasted_iota(jnp.int32, (8 * ny, 1), 0)
        onehot = jnp.where(unknown == owners, 1.0, 0.0).astype(BF16)
        values(4)
        parts = jnp.zeros((RHS, 128), F32)
        for s in range(SUBS):
            for f in range(6):
                parts += value_of(s, f, f, s)
            if s < SUBS - 1:
                parts -= value_of(s + 1, 5, 4, s)
            if s > 0:
                parts -= value_of(s - 1, 4, 5, s)

    with jax.named_scope("wait_values"):
        arrivals[0]("wait_recv")

    with jax.named_scope("corners"):
        for f in range(4):
            received = y_in[f]
            slots = jnp.zeros((1, 128), jnp.int32)
            for s in range(SUBS):
                slots = jnp.where(block == s, partner[s, f], slots)
            for d in range(SUBS):
                here = slots == lax.rem(block - d + SUBS, SUBS)
                parts -= jnp.where(here, moved(received, d), 0.0)
        parts = parts * visc_lanes
        comp = lax.rem(lax.rem(lane, BLOCK), COMPS)
        for c in range(COMPS):
            stacked[pl.ds(c, RHS, stride=COMPS)] = jnp.where(comp == c, parts, 0.0)
        pieces = split(stacked[...], 3)

    def assemble(first, last):
        total = sum(nt_dot(onehot[first * 8 : last * 8], piece) for piece in pieces)
        total = total.reshape(last - first, 8, RHS * COMPS)
        pad = jnp.zeros((last - first, 8, 128 - RHS * COMPS), F32)
        total = jnp.concatenate([total, pad], 2)
        for to in range(first, last):
            tile = total[to - first]
            dense[to] = jnp.where(lane < 64, tile[:4], pltpu.roll(tile[4:], 64, 1))

    def corner_copy(to):
        return pltpu.make_async_remote_copy(
            src_ref=dense.at[to],
            dst_ref=z_in.at[sy],
            send_sem=share_sem.at[0],
            recv_sem=share_sem.at[1],
            device_id=(sx, to),
            device_id_type=MESH,
        )

    shares = pltpu.make_async_remote_copy(
        src_ref=dense.at[pl.ds(0, ny - 1)],
        dst_ref=z_in.at[pl.ds(0, ny - 1)],
        send_sem=share_sem.at[0],
        recv_sem=share_sem.at[1],
        device_id=beside[0],
        device_id_type=MESH,
    )

    with jax.named_scope("corner_send"):
        assemble(0, FIRST)
        to_others(0, jnp.minimum(known, FIRST), lambda to: corner_copy(to).start())
    pl.when(z >= ny // QUAD // 2)(send_traces)
    if FIRST < ny:
        with jax.named_scope("corner_rest"):
            assemble(FIRST, ny)
            to_others(FIRST, known, lambda to: corner_copy(to).start())

    def selected(f, received):
        received = received.astype(F32)
        slots = [received[p * HALF : (p + 1) * HALF] for p in range(SUBS)]
        values = []
        for s in range(SUBS):
            value = slots[0]
            for p in range(1, SUBS):
                value = jnp.where(partner[s, f] == p, slots[p], value)
            values.append(value)
        return jnp.concatenate(values, 0)

    none = jnp.zeros((HALF, width), F32)
    visc_rows = jnp.concatenate([jnp.full((HALF, width), visc[s], F32) for s in range(SUBS)], 0)
    size = SUBS * HALF

    for c in range(2):
        with jax.named_scope(f"wait_traces{c}"):
            arrivals[1 + c]("wait_recv")
        with jax.named_scope(f"local{c}"):
            for f in range(4):
                mine = own[c, f].reshape(size, width)
                jump[f * size : (f + 1) * size] = (mine - selected(f, in1[c, f])).astype(BF16)
            top, bottom = own[c, 4].reshape(size, width), own[c, 5].reshape(size, width)
            above = jnp.concatenate([bottom[HALF:], none], 0)
            below = jnp.concatenate([none, top[:-HALF]], 0)
            jump[4 * size : 5 * size] = (top - above).astype(BF16)
            jump[5 * size : 6 * size] = (bottom - below).astype(BF16)
            w_c[...] = jnp.dot(jump[...], c_mat[...], preferred_element_type=F32)
            w_s[...] = jnp.dot(jump[...], s_mat[...], preferred_element_type=F32)
            w_o[...] = jnp.dot(jump[...], o_mat[...], preferred_element_type=F32)

            def face(ref, f):
                return ref[f * size : (f + 1) * size]

            for f in range(6):
                others = [g for g in range(6) if g // 2 != f // 2]
                value = face(w_s, f) + face(w_o, OPP[f])
                value += (face(w_c, others[0]) + face(w_c, others[1])) + (
                    face(w_c, others[2]) + face(w_c, others[3])
                )
                local[c, f] = (visc_rows * value).astype(BF16)
                if f < 4:
                    exchange(*steps[3 + c], f)
            top, bottom = local[c, 4].astype(F32), local[c, 5].astype(F32)
            above = jnp.concatenate([bottom[HALF:], none], 0)
            below = jnp.concatenate([none, top[:-HALF]], 0)
            for f, value in ((4, top - above), (5, bottom - below)):
                for s in range(SUBS):
                    applied[0, 0, s, f, c * HALF : (c + 1) * HALF] = value[s * HALF : (s + 1) * HALF]

    def finish(c):
        with jax.named_scope(f"wait_local{c}"):
            arrivals[3 + c]("wait_recv")
        with jax.named_scope(f"applied{c}"):
            for f in range(4):
                value = local[c, f].astype(F32) - selected(f, in2[c, f])
                for s in range(SUBS):
                    applied[0, 0, s, f, c * HALF : (c + 1) * HALF] = value[s * HALF : (s + 1) * HALF]

    with jax.named_scope("far"):
        pl.when(known < ny)(lambda: pl.semaphore_wait(far_sem, ny - known))
        to_others(known, ny, lambda to: corner_copy(to).start())

    finish(0)
    finish(1)

    with jax.named_scope("corner_wait"):
        shares.wait_recv()
    with jax.named_scope("corner_sum"):
        result = jnp.zeros((4, 128), F32)
        for source in range(ny):
            result += jnp.where(sy == source, dense[source], z_in[source])
        coarse[:4] = result[:, : RHS * COMPS]
        coarse[4:] = pltpu.roll(result, 64, 1)[:, : RHS * COMPS]

    with jax.named_scope("sent"):
        shares.wait_send()
        for wait in arrivals:
            wait("wait_send")


def write_out(applied, coarse, applied_out, coarse_out, sems):
    copies = [pltpu.make_async_copy(coarse, coarse_out, sems.at[SUBS])]
    for s in range(SUBS):
        copies.append(pltpu.make_async_copy(applied.at[0, 0, s], applied_out.at[0, 0, s], sems.at[s]))
    for copy in copies:
        copy.start()
    for copy in copies:
        copy.wait()


def body(traces, viscosity, partner, corner_owner, self_block, opposite_block, cross_block, corner_map):
    nx, ny = lax.axis_size("sx"), lax.axis_size("sy")
    width = traces.shape[-1]
    vmem, dma = pltpu.VMEM, pltpu.SemaphoreType.DMA
    size = SUBS * HALF
    inputs = (
        traces, viscosity, partner, corner_owner, self_block, opposite_block, cross_block,
        jnp.transpose(corner_map, (1, 0, 2)),
    )
    inputs = [pltpu.with_memory_space_constraint(value, pltpu.HBM) for value in inputs]
    applied, coarse = pl.pallas_call(
        functools.partial(kernel, nx, ny),
        out_shape=(
            jax.ShapeDtypeStruct(traces.shape, F32),
            jax.ShapeDtypeStruct((8, RHS * COMPS), F32),
        ),
        in_specs=[pl.BlockSpec(memory_space=pltpu.HBM)] * 8,
        out_specs=(pl.BlockSpec(memory_space=vmem), pl.BlockSpec(memory_space=vmem)),
        scratch_shapes=[
            vmem((SUBS, 6, RHS, width), BF16),
            vmem((width, width), BF16),
            vmem((width, width), BF16),
            vmem((width, width), BF16),
            vmem((6, KEYS, width), BF16),
            pltpu.SMEM((SUBS,), F32),
            pltpu.SMEM((SUBS, 4), jnp.int32),
            pltpu.SMEM((SUBS, CORNERS), jnp.int32),
            vmem((2, 6, SUBS, HALF, width), F32),
            vmem((2, 4, size, width), BF16),
            vmem((2, 4, size, width), BF16),
            vmem((6 * size, width), BF16),
            vmem((6 * size, width), F32),
            vmem((6 * size, width), F32),
            vmem((6 * size, width), F32),
            vmem((2, 6, size, width), BF16),
            vmem((2, 4, size, width), BF16),
            vmem((8 * BLOCK, width), BF16),
            vmem((8 * BLOCK, width), BF16),
            vmem((SUBS, 6, RHS, 8 * BLOCK), F32),
            vmem((4, RHS, 128), F32),
            vmem((4, RHS, 128), F32),
            vmem((RHS * COMPS, 128), F32),
            vmem((ny, 4, 128), F32),
            vmem((ny, 4, 128), F32),
            dma((8,)),
            dma((5,)),
            dma((5,)),
            dma((2,)),
            pltpu.SemaphoreType.REGULAR,
        ],
        compiler_params=pltpu.CompilerParams(
            collective_id=0, has_side_effects=True, vmem_limit_bytes=40 * 2**20
        ),
    )(*inputs)
    applied, coarse = pl.pallas_call(
        write_out,
        out_shape=tuple(jax.ShapeDtypeStruct(value.shape, F32) for value in (applied, coarse)),
        in_specs=[pl.BlockSpec(memory_space=pltpu.VMEM)] * 2,
        out_specs=(pl.BlockSpec(memory_space=pltpu.HBM),) * 2,
        scratch_shapes=[dma((SUBS + 1,))],
    )(*(pltpu.with_memory_space_constraint(value, pltpu.VMEM) for value in (applied, coarse)))
    return applied, coarse.T


def solution(mesh):
    return jax.shard_map(
        body,
        mesh=mesh,
        in_specs=(
            P("sx", "sy", None, None, None, None),
            P("sx", "sy", None),
            P("sx", "sy", None, None),
            P("sx", "sy", None, None),
            P(),
            P(),
            P(),
            P(),
        ),
        out_specs=(P("sx", "sy", None, None, None, None), P(None, ("sx", "sy"))),
        check_vma=False,
    )
```

```python
import functools

import jax
import jax.numpy as jnp
from jax import lax
from jax.experimental import pallas as pl
from jax.experimental.pallas import tpu as pltpu
from jax.sharding import PartitionSpec as P

MESH = pl.DeviceIdType.MESH
F32, BF16 = jnp.float32, jnp.bfloat16
SUBS = 4
RHS = 16
HALF = 8
CORNERS = 8
COMPS = 3
KEYS = CORNERS * COMPS
BLOCK = 32
QUAD = 4
OPP = (1, 0, 3, 2, 5, 4)
FIRST = 3 * QUAD


def nt_dot(left, right):
    return lax.dot_general(left, right, (((1,), (1,)), ((), ())), preferred_element_type=F32)


def split(value, parts):
    out = []
    for _ in range(parts):
        head = value.astype(BF16)
        out.append(head)
        value = value - head.astype(F32)
    return out


def kernel(
    nx, ny,
    traces, visc_in, partner_in, owner_in, self_in, opp_in, cross_in, cmap_in,
    applied, coarse,
    raw, s_mat, o_mat, c_mat, cmap, visc, partner, owner,
    own, out1, in1, jump, w_s, w_o, w_c, local, in2,
    w_hi, w_lo, y_all, y_out, y_in, stacked, dense, z_in,
    load_sem, send, recv, share_sem, far_sem,
):
    width = raw.shape[-1]
    sx, sy = lax.axis_index("sx"), lax.axis_index("sy")
    z = sy // QUAD

    def in_row(to):
        return (sx, lax.rem(to + ny, ny))

    beside = (
        (lax.rem(sx + 1, nx), sy),
        (lax.rem(sx + nx - 1, nx), sy),
        in_row(sy + 1),
        in_row(sy - 1),
    )
    inside = (sx < nx - 1, sx > 0, sy < ny - 1, sy > 0)

    barrier = pltpu.get_barrier_semaphore()

    def signal(semaphore, device):
        pl.semaphore_signal(semaphore, inc=1, device_id=device, device_id_type=MESH)

    with jax.named_scope("greet"):
        for f in range(4):
            pl.when(inside[f])(functools.partial(signal, barrier, beside[f]))

    loads = {}
    for i, (name, source, target) in enumerate((
        ("cmap", cmap_in, cmap),
        ("cross", cross_in, c_mat),
        ("self", self_in, s_mat),
        ("opp", opp_in, o_mat),
        ("raw", traces.at[0, 0], raw),
        ("visc", visc_in.at[0, 0], visc),
        ("partner", partner_in.at[0, 0], partner),
        ("owner", owner_in.at[0, 0], owner),
    )):
        loads[name] = pltpu.make_async_copy(source, target, load_sem.at[i])
        loads[name].start()

    known = (z + 1) * QUAD

    def to_others(first, last, act):
        @pl.loop(first, last)
        def _(to):
            pl.when(to != sy)(lambda: act(to))

    with jax.named_scope("greet_row"):
        to_others(z * QUAD, ny, lambda to: signal(barrier, (sx, to)))

    count = sum(here.astype(jnp.int32) for here in inside)

    def exchange(step, source, target, f):
        copy = pltpu.make_async_remote_copy(
            src_ref=source.at[f],
            dst_ref=target.at[OPP[f]],
            send_sem=send.at[step],
            recv_sem=recv.at[step],
            device_id=beside[f],
            device_id_type=MESH,
        )
        pl.when(inside[f])(copy.start)

    def arrival(step, source, target):
        copies = [
            pltpu.make_async_remote_copy(
                src_ref=source.at[pl.ds(0, k)],
                dst_ref=target.at[pl.ds(0, k)],
                send_sem=send.at[step],
                recv_sem=recv.at[step],
                device_id=beside[0],
                device_id_type=MESH,
            )
            for k in (2, 3, 4)
        ]

        def wait(which):
            for k, copy in zip((2, 3, 4), copies):
                pl.when(count == k)(getattr(copy, which))

        return wait

    steps = [
        (0, y_out, y_in),
        (1, out1.at[0], in1.at[0]),
        (2, out1.at[1], in1.at[1]),
        (3, local.at[0], in2.at[0]),
        (4, local.at[1], in2.at[1]),
    ]
    arrivals = [arrival(*step) for step in steps]

    lane = lax.broadcasted_iota(jnp.int32, (1, 128), 1)
    block = lane // BLOCK

    def moved(value, shift):
        shift = (shift * BLOCK) % 128
        return pltpu.roll(value, shift, 1) if shift else value

    with jax.named_scope("corner_map"):
        loads["cmap"].wait()
        pad = jnp.zeros((BLOCK - KEYS, width), F32)
        faces = [jnp.concatenate([cmap[f].astype(F32), pad], 0) for f in range(6)]
        straight = jnp.concatenate(faces, 0).astype(BF16)

    def through(rows, matrix):
        product = nt_dot(rows, matrix[...])
        return [product[at : at + BLOCK] for at in range(0, rows.shape[0], BLOCK)]

    half = 4 * BLOCK
    with jax.named_scope("weights_cross"):
        loads["cross"].wait()
        cross = through(straight, c_mat)
    with jax.named_scope("weights_self"):
        loads["self"].wait()
        same = through(straight[:half], s_mat)
    with jax.named_scope("weights_opposite"):
        loads["opp"].wait()
        across = through(straight[:half], o_mat)
        pairs = [cross[0] + cross[1], cross[2] + cross[3], cross[4] + cross[5]]
        adjacent = [pairs[1] + pairs[2], pairs[0] + pairs[2], pairs[0] + pairs[1]]
        weight = [same[f] + across[OPP[f]] + adjacent[f // 2] for f in range(4)]
        w_hi[:half], w_lo[:half] = split(jnp.concatenate(weight, 0), 2)

    def z_weights():
        same, across = through(straight[half:], s_mat), through(straight[half:], o_mat)
        weight = [same[f] + across[1 - f] + adjacent[2] for f in range(2)]
        weight.append(jnp.zeros((2 * BLOCK, width), F32))
        w_hi[half:], w_lo[half:] = split(jnp.concatenate(weight, 0), 2)

    def value_of(s, f, face, to):
        return jnp.where(block == to, moved(y_all[s, f], to - face % 4), 0.0)

    def values(f):
        flat = raw[:, f : f + 2].reshape(SUBS * 2 * RHS, width)
        rows = pl.ds(f // 4 * half, half)
        both = nt_dot(flat, w_hi[rows]) + nt_dot(flat, w_lo[rows])
        y_all[:, f : f + 2] = both.reshape(SUBS, 2, RHS, half)

    for f in (0, 2):
        with jax.named_scope(f"values{f}"):
            if f == 0:
                loads["raw"].wait()
            values(f)
            for to in (f, f + 1):
                y_out[to] = sum(value_of(s, to, OPP[to], s) for s in range(SUBS))
        if f == 0:
            with jax.named_scope("entry"):
                pl.semaphore_wait(barrier, count + known - 1)
        for to in (f, f + 1):
            exchange(*steps[0], to)

    with jax.named_scope("repack"):
        for f in range(6):
            for s in range(SUBS):
                both = raw[s, f].astype(F32)
                for c in range(2):
                    own[c, f, s] = both[c * HALF : (c + 1) * HALF]
            if f < 4:
                for c in range(2):
                    out1[c, f] = own[c, f].reshape(SUBS * HALF, width).astype(BF16)

    def send_traces():
        for c in range(2):
            for f in range(4):
                exchange(*steps[1 + c], f)

    pl.when(z < ny // QUAD // 2)(send_traces)
    to_others(0, z * QUAD, lambda to: signal(far_sem, (sx, to)))

    for f in range(4):
        def clear(f=f):
            y_in[f] = jnp.zeros(y_in.shape[1:], F32)
            for ref in (in1, in2):
                for c in range(2):
                    ref[c, f] = jnp.zeros(ref.shape[2:], BF16)

        pl.when(jnp.logical_not(inside[f]))(clear)

    with jax.named_scope("owners"):
        for name in ("visc", "partner", "owner"):
            loads[name].wait()
        visc_lanes = jnp.zeros((1, 128), F32)
        for s in range(SUBS):
            visc_lanes = jnp.where(block == s, visc[s], visc_lanes)
        owners = jnp.full((1, 128), -1, jnp.int32)
        for s in range(SUBS):
            for m in range(CORNERS):
                first = s * BLOCK + m * COMPS
                owners = jnp.where((lane >= first) & (lane < first + COMPS), owner[s, m], owners)
        unknown = lax.broadcasted_iota(jnp.int32, (8 * ny, 1), 0)
        onehot = jnp.where(unknown == owners, 1.0, 0.0).astype(BF16)
        z_weights()
        values(4)
        parts = jnp.zeros((RHS, 128), F32)
        for s in range(SUBS):
            for f in range(6):
                parts += value_of(s, f, f, s)
            if s < SUBS - 1:
                parts -= value_of(s + 1, 5, 4, s)
            if s > 0:
                parts -= value_of(s - 1, 4, 5, s)

    with jax.named_scope("wait_values"):
        arrivals[0]("wait_recv")

    with jax.named_scope("corners"):
        for f in range(4):
            received = y_in[f]
            slots = jnp.zeros((1, 128), jnp.int32)
            for s in range(SUBS):
                slots = jnp.where(block == s, partner[s, f], slots)
            for d in range(SUBS):
                here = slots == lax.rem(block - d + SUBS, SUBS)
                parts -= jnp.where(here, moved(received, d), 0.0)
        parts = parts * visc_lanes
        comp = lax.rem(lax.rem(lane, BLOCK), COMPS)
        for c in range(COMPS):
            stacked[pl.ds(c, RHS, stride=COMPS)] = jnp.where(comp == c, parts, 0.0)
        pieces = split(stacked[...], 2)

    def assemble(first, last):
        total = sum(nt_dot(onehot[first * 8 : last * 8], piece) for piece in pieces)
        total = total.reshape(last - first, 8, RHS * COMPS)
        pad = jnp.zeros((last - first, 8, 128 - RHS * COMPS), F32)
        total = jnp.concatenate([total, pad], 2)
        for to in range(first, last):
            tile = total[to - first]
            dense[to] = jnp.where(lane < 64, tile[:4], pltpu.roll(tile[4:], 64, 1))

    def corner_copy(to):
        return pltpu.make_async_remote_copy(
            src_ref=dense.at[to],
            dst_ref=z_in.at[sy],
            send_sem=share_sem.at[0],
            recv_sem=share_sem.at[1],
            device_id=(sx, to),
            device_id_type=MESH,
        )

    shares = pltpu.make_async_remote_copy(
        src_ref=dense.at[pl.ds(0, ny - 1)],
        dst_ref=z_in.at[pl.ds(0, ny - 1)],
        send_sem=share_sem.at[0],
        recv_sem=share_sem.at[1],
        device_id=beside[0],
        device_id_type=MESH,
    )

    with jax.named_scope("corner_send"):
        assemble(0, FIRST)
        to_others(0, jnp.minimum(known, FIRST), lambda to: corner_copy(to).start())
    pl.when(z >= ny // QUAD // 2)(send_traces)
    if FIRST < ny:
        with jax.named_scope("corner_rest"):
            assemble(FIRST, ny)
            to_others(FIRST, known, lambda to: corner_copy(to).start())

    def selected(f, received):
        received = received.astype(F32)
        slots = [received[p * HALF : (p + 1) * HALF] for p in range(SUBS)]
        values = []
        for s in range(SUBS):
            value = slots[0]
            for p in range(1, SUBS):
                value = jnp.where(partner[s, f] == p, slots[p], value)
            values.append(value)
        return jnp.concatenate(values, 0)

    none = jnp.zeros((HALF, width), F32)
    visc_rows = jnp.concatenate([jnp.full((HALF, width), visc[s], F32) for s in range(SUBS)], 0)
    size = SUBS * HALF

    for c in range(2):
        with jax.named_scope(f"wait_traces{c}"):
            arrivals[1 + c]("wait_recv")
        with jax.named_scope(f"local{c}"):
            for f in range(4):
                mine = own[c, f].reshape(size, width)
                jump[f * size : (f + 1) * size] = (mine - selected(f, in1[c, f])).astype(BF16)
            top, bottom = own[c, 4].reshape(size, width), own[c, 5].reshape(size, width)
            above = jnp.concatenate([bottom[HALF:], none], 0)
            below = jnp.concatenate([none, top[:-HALF]], 0)
            jump[4 * size : 5 * size] = (top - above).astype(BF16)
            jump[5 * size : 6 * size] = (bottom - below).astype(BF16)
            w_c[...] = jnp.dot(jump[...], c_mat[...], preferred_element_type=F32)
            w_s[...] = jnp.dot(jump[...], s_mat[...], preferred_element_type=F32)
            w_o[...] = jnp.dot(jump[...], o_mat[...], preferred_element_type=F32)

            def face(ref, f):
                return ref[f * size : (f + 1) * size]

            for f in range(6):
                others = [g for g in range(6) if g // 2 != f // 2]
                value = face(w_s, f) + face(w_o, OPP[f])
                value += (face(w_c, others[0]) + face(w_c, others[1])) + (
                    face(w_c, others[2]) + face(w_c, others[3])
                )
                local[c, f] = (visc_rows * value).astype(BF16)
                if f < 4:
                    exchange(*steps[3 + c], f)
            top, bottom = local[c, 4].astype(F32), local[c, 5].astype(F32)
            above = jnp.concatenate([bottom[HALF:], none], 0)
            below = jnp.concatenate([none, top[:-HALF]], 0)
            for f, value in ((4, top - above), (5, bottom - below)):
                for s in range(SUBS):
                    applied[0, 0, s, f, c * HALF : (c + 1) * HALF] = value[s * HALF : (s + 1) * HALF]

    def finish(c):
        with jax.named_scope(f"wait_local{c}"):
            arrivals[3 + c]("wait_recv")
        with jax.named_scope(f"applied{c}"):
            for f in range(4):
                value = local[c, f].astype(F32) - selected(f, in2[c, f])
                for s in range(SUBS):
                    applied[0, 0, s, f, c * HALF : (c + 1) * HALF] = value[s * HALF : (s + 1) * HALF]

    with jax.named_scope("far"):
        pl.when(known < ny)(lambda: pl.semaphore_wait(far_sem, ny - known))
        to_others(known, ny, lambda to: corner_copy(to).start())

    finish(0)
    finish(1)

    with jax.named_scope("corner_wait"):
        shares.wait_recv()
    with jax.named_scope("corner_sum"):
        result = jnp.zeros((4, 128), F32)
        for source in range(ny):
            result += jnp.where(sy == source, dense[source], z_in[source])
        coarse[:4] = result[:, : RHS * COMPS]
        coarse[4:] = pltpu.roll(result, 64, 1)[:, : RHS * COMPS]

    with jax.named_scope("sent"):
        shares.wait_send()
        for wait in arrivals:
            wait("wait_send")


def write_out(applied, coarse, applied_out, coarse_out, sems):
    copies = [pltpu.make_async_copy(coarse, coarse_out, sems.at[SUBS])]
    for s in range(SUBS):
        copies.append(pltpu.make_async_copy(applied.at[0, 0, s], applied_out.at[0, 0, s], sems.at[s]))
    for copy in copies:
        copy.start()
    for copy in copies:
        copy.wait()


def body(traces, viscosity, partner, corner_owner, self_block, opposite_block, cross_block, corner_map):
    nx, ny = lax.axis_size("sx"), lax.axis_size("sy")
    width = traces.shape[-1]
    vmem, dma = pltpu.VMEM, pltpu.SemaphoreType.DMA
    size = SUBS * HALF
    inputs = (
        traces, viscosity, partner, corner_owner, self_block, opposite_block, cross_block,
        jnp.transpose(corner_map, (1, 0, 2)),
    )
    inputs = [pltpu.with_memory_space_constraint(value, pltpu.HBM) for value in inputs]
    applied, coarse = pl.pallas_call(
        functools.partial(kernel, nx, ny),
        out_shape=(
            jax.ShapeDtypeStruct(traces.shape, F32),
            jax.ShapeDtypeStruct((8, RHS * COMPS), F32),
        ),
        in_specs=[pl.BlockSpec(memory_space=pltpu.HBM)] * 8,
        out_specs=(pl.BlockSpec(memory_space=vmem), pl.BlockSpec(memory_space=vmem)),
        scratch_shapes=[
            vmem((SUBS, 6, RHS, width), BF16),
            vmem((width, width), BF16),
            vmem((width, width), BF16),
            vmem((width, width), BF16),
            vmem((6, KEYS, width), BF16),
            pltpu.SMEM((SUBS,), F32),
            pltpu.SMEM((SUBS, 4), jnp.int32),
            pltpu.SMEM((SUBS, CORNERS), jnp.int32),
            vmem((2, 6, SUBS, HALF, width), F32),
            vmem((2, 4, size, width), BF16),
            vmem((2, 4, size, width), BF16),
            vmem((6 * size, width), BF16),
            vmem((6 * size, width), F32),
            vmem((6 * size, width), F32),
            vmem((6 * size, width), F32),
            vmem((2, 6, size, width), BF16),
            vmem((2, 4, size, width), BF16),
            vmem((8 * BLOCK, width), BF16),
            vmem((8 * BLOCK, width), BF16),
            vmem((SUBS, 6, RHS, 4 * BLOCK), F32),
            vmem((4, RHS, 128), F32),
            vmem((4, RHS, 128), F32),
            vmem((RHS * COMPS, 128), F32),
            vmem((ny, 4, 128), F32),
            vmem((ny, 4, 128), F32),
            dma((8,)),
            dma((5,)),
            dma((5,)),
            dma((2,)),
            pltpu.SemaphoreType.REGULAR,
        ],
        compiler_params=pltpu.CompilerParams(
            collective_id=0, has_side_effects=True, vmem_limit_bytes=40 * 2**20
        ),
    )(*inputs)
    applied, coarse = pl.pallas_call(
        write_out,
        out_shape=tuple(jax.ShapeDtypeStruct(value.shape, F32) for value in (applied, coarse)),
        in_specs=[pl.BlockSpec(memory_space=pltpu.VMEM)] * 2,
        out_specs=(pl.BlockSpec(memory_space=pltpu.HBM),) * 2,
        scratch_shapes=[dma((SUBS + 1,))],
    )(*(pltpu.with_memory_space_constraint(value, pltpu.VMEM) for value in (applied, coarse)))
    return applied, coarse.T


def solution(mesh):
    return jax.shard_map(
        body,
        mesh=mesh,
        in_specs=(
            P("sx", "sy", None, None, None, None),
            P("sx", "sy", None),
            P("sx", "sy", None, None),
            P("sx", "sy", None, None),
            P(),
            P(),
            P(),
            P(),
        ),
        out_specs=(P("sx", "sy", None, None, None, None), P(None, ("sx", "sy"))),
        check_vma=False,
    )
```
